512 devices in a mesh: batch: 16 (over y, z_hi), proto: 32 (over x, z_lo, core).
Axes of the slice: x: 4, y: 4, z: 16 (z_hi: 4, z_lo: 4; z = z_hi * 4 + z_lo), core: 2. Of those that a mesh axis runs over, the one named last changes fastest.
Arguments:
- teacher_feats: bfloat16 [8192, 1536], P('batch'), may hold values from -8 to 8
- teacher_weight: bfloat16 [1536, 32768], P('batch', 'proto'), may hold values from -1 to 1
- student_feats: bfloat16 [8192, 1024], P('batch'), may hold values from -6 to 6
- student_weight: bfloat16 [1024, 32768], P('batch', 'proto'), may hold values from -3 to 3
Outputs:
- loss: float32 [], replicated
- grad_student_weight: bfloat16 [1024, 32768], P('batch', 'proto')
- grad_student_feats: bfloat16 [8192, 1024], P('batch')
The draws below stay inside these ranges and needn't reach their ends.
All inputs are finite; a program needn't handle non-finite values.
Results may differ from the reference program's by a relative error of at most 0.0082.
Values may be sent and summed in bfloat16 or wider, within the bound.
A program may use at most 64 MiB of HBM per device.

```python
import jax
import jax.numpy as jnp
from jax import lax

DT = 1536
DS = 1024
K = 32768
ROUNDS = 3
TOK = 8192


def draw_teacher_feats(key, part):
    key = jax.random.fold_in(key, 11)
    first_key, second_key = jax.random.split(key)
    random_part = jax.random.truncated_normal(first_key, -4.0, 4.0, (TOK, DT), jnp.float32)
    latent = jax.random.uniform(second_key, (TOK, 2), jnp.float32, -1.7, 1.7)
    parity = jnp.arange(DT) % 2
    spread = jnp.where(parity[None, :] == 0, latent[:, 0:1], latent[:, 1:2])
    return (random_part + 0.7 * spread).astype(jnp.bfloat16)


def draw_teacher_weight(key, part):
    key = jax.random.fold_in(key, 12)
    first_key, second_key = jax.random.split(key)
    random_part = 0.1 * jax.random.truncated_normal(first_key, -4.0, 4.0, (DT, K), jnp.float32)
    latent = jax.random.uniform(second_key, (K, 2), jnp.float32, -1.7, 1.7)
    latent_coef = 2.0
    parity = jnp.arange(DT) % 2
    spread = jnp.where(parity[:, None] == 0, latent[None, :, 0], latent[None, :, 1])
    return (random_part + latent_coef * DT ** (-0.5) * spread).astype(jnp.bfloat16)


def shard_levels(stream_key, extent, cuts, low, largest):
    level = 1.0
    for position, parts in cuts:
        draws = jax.random.uniform(jax.random.fold_in(jax.random.fold_in(stream_key, 6), position), (parts,), jnp.float32, low / len(cuts), largest / len(cuts))
        level = level * jnp.repeat(jnp.exp(draws), extent[position] // parts).reshape((-1,) + (1,) * (len(extent) - 1 - position))
    return level


def bell_draw(key, extent, deviation, reach, pieces=(), dtype=jnp.bfloat16):
    array = deviation * jax.random.normal(key, extent, jnp.float32)
    if pieces:
        array = array * shard_levels(key, extent, pieces, -0.22, 0.18)
    return jnp.clip(array, -reach, reach).astype(dtype)


def setup_inputs(seed: int = 0) -> dict:
    seeds = jax.random.split(jax.random.key(seed), 5)
    return {
        "teacher_feats": draw_teacher_feats(jax.random.fold_in(seeds[4], 71), 0),
        "teacher_weight": draw_teacher_weight(jax.random.fold_in(seeds[4], 71), 0),
        "student_feats": bell_draw(seeds[2], (TOK, DS), 1.0, 6.0, ((0, 16),)),
        "student_weight": bell_draw(seeds[3], (DS, K), (6.4 * DS ** -0.5), 3.0, ((0, 16), (1, 32))),
    }


teacher_temp = 0.07
student_temp = 0.1
loss_scale = 1024.0

def unit_rows(values):
    wide = values.astype(jnp.float32)
    scale = lax.rsqrt(lax.optimization_barrier(jnp.sum(wide * wide, axis=1, keepdims=True)) + 1e-06)
    return (wide * scale, scale)

def reference(teacher_feats, teacher_weight, student_feats, student_weight):
    teacher_unit, _ = unit_rows(teacher_feats)
    scores = jnp.dot(teacher_unit.astype(jnp.bfloat16), teacher_weight, preferred_element_type=jnp.float32)
    mass = jnp.exp(scores / teacher_temp)
    crops = mass.shape[0]
    protos = mass.shape[1]
    for step in range(ROUNDS):
        mass = mass / (protos * lax.optimization_barrier(jnp.sum(mass, axis=0, keepdims=True)))
        mass = mass / (crops * lax.optimization_barrier(jnp.sum(mass, axis=1, keepdims=True)))
    targets = (mass * crops).astype(jnp.bfloat16)
    relayed = jnp.roll(targets, crops // 2, axis=0).astype(jnp.float32)
    student_unit, scale = unit_rows(student_feats)
    student_half = student_unit.astype(jnp.bfloat16)
    logits = jnp.dot(student_half, student_weight, preferred_element_type=jnp.float32) / student_temp
    expo = jnp.exp(logits)
    total = lax.optimization_barrier(jnp.sum(expo, axis=1))
    weight_sum = lax.optimization_barrier(jnp.sum(relayed, axis=1))
    loss = jnp.sum(weight_sum * jnp.log(total) - lax.optimization_barrier(jnp.sum(relayed * logits, axis=1))) / crops
    slope = (loss_scale * (weight_sum[:, None] * expo / total[:, None] - relayed) / student_temp).astype(jnp.bfloat16)
    grad_weight = jnp.dot(student_half.T, slope, preferred_element_type=jnp.float32).astype(jnp.bfloat16)
    back = jnp.dot(slope, student_weight.T, preferred_element_type=jnp.float32)
    inner = lax.optimization_barrier(jnp.sum(student_unit * back, axis=1, keepdims=True))
    grad_feats = ((back - student_unit * inner) * scale).astype(jnp.bfloat16)
    return (loss, grad_weight, grad_feats)
```

```python
import jax
import jax.numpy as jnp
from jax import lax
from jax.experimental import pallas as pl
from jax.experimental.pallas import tpu as pltpu
from jax.sharding import PartitionSpec as P

F32 = jnp.float32
BF16 = jnp.bfloat16
MESH = pl.DeviceIdType.MESH

TEACHER_TEMP = 0.07
STUDENT_TEMP = 0.1
LOSS_SCALE = 1024.0
CROPS = 8192.0
PROTOS = 32768.0
GAIN = LOSS_SCALE / STUDENT_TEMP

ROWS = 512
COLS = 1024
DT = 1536
DS = 1024
NSEM = 160


def device(y, zh, x, zl, c):
    return (y * 4 + zh, (x * 4 + zl) * 2 + c)


def nt(a, b):
    return lax.dot_general(a, b, (((1,), (1,)), ((), ())), preferred_element_type=F32)


def lanes(part):
    ones = jnp.ones((8, 128), F32)
    out = lax.dot_general(
        ones, part, (((1,), (1,)), ((), ())),
        precision=lax.Precision.HIGHEST, preferred_element_type=F32,
    )
    return out[0:1, :]


def inverse(value, gain):
    part = jnp.where(value > 1.0, 0.25, 1.0)
    return (1.0 / (value * part)) * (part * gain)


def kernel(
    tf, tw, sf, sw, loss_out, gw_out, gf_out,
    tu, wt, ws, sf2, sh, sht, mass, logit, expo, slope,
    rowpart, totpart, rowb, probb,
    colmsg, colbuf, rowmsg, rowbuf, lastmsg, lastbuf,
    lossmsg, lossrow, losscol,
    bsend, bown, brecv, xsend, xrecv, lsend, lrecv, gfin, gfs,
    gsend, gown, grecv, zsend, zown, zrecv,
    ssem, rsem,
):
    b = lax.axis_index("batch")
    p = lax.axis_index("proto")
    y, zh = b // 4, b % 4
    x, zl, c = p // 8, (p // 2) % 4, p % 2

    def at_y(d):
        return lax.rem(y + d, 4)

    def at_zh(d):
        return lax.rem(zh + d, 4)

    def at_x(d):
        return lax.rem(x + d, 4)

    used = [0]
    pending = []

    def sem():
        used[0] += 1
        return used[0] - 1

    def send(src, dst, dev, s=None, r=None):
        s = sem() if s is None else s
        r = s if r is None else r
        copy = pltpu.make_async_remote_copy(
            src_ref=src, dst_ref=dst, send_sem=ssem.at[s], recv_sem=rsem.at[r],
            device_id=dev, device_id_type=MESH,
        )
        copy.start()
        return copy

    def single(src, dst, dev):
        copy = send(src, dst, dev)
        pending.append(copy.wait_send)
        return copy

    def wait_bytes(ref, s):
        pltpu.make_async_copy(ref, ref, s).wait()

    def batch_send(src, buf):
        s = sem()
        for dz in (2, 1, 3, 0):
            for dy in (2, 1, 3, 0):
                if dy or dz:
                    send(src, buf.at[dy * 4 + dz - 1], device(at_y(dy), at_zh(dz), x, zl, c), s)
        pending.append(lambda: wait_bytes(buf, ssem.at[s]))
        return lambda: wait_bytes(buf, rsem.at[s])

    def proto_send(src, buf):
        s = sem()

        def body(i, carry):
            k = 31 - i
            dx, dl, dc = k // 8, (k // 2) % 4, k % 2
            fl = lax.rem(zl + dl, 4)
            send(src, buf.at[k - 1], device(y, zh, at_x(dx), fl, lax.rem(c + dc, 2)), s)
            return carry

        lax.fori_loop(0, 31, body, 0)
        pending.append(lambda: wait_bytes(buf, ssem.at[s]))
        return lambda: wait_bytes(buf, rsem.at[s])

    near = [device(at_y(d), zh, x, zl, c) for d in (1, 2, 3)]
    near += [device(y, at_zh(d), x, zl, c) for d in (1, 2, 3)]
    near += [device(y, zh, x, lax.rem(zl + d, 4), c) for d in (1, 2, 3)]
    near += [
        device(y, zh, at_x(d), zl, lax.rem(c + e, 2))
        for d in range(4) for e in range(2) if d or e
    ]
    barrier = pltpu.get_barrier_semaphore()
    for dev in near:
        pl.semaphore_signal(barrier, inc=1, device_id=dev, device_id_type=MESH)

    def own(block, size):
        return pl.ds(pl.multiple_of(block * size, 16), size)

    wt[own(b, 96), :] = tw[...]
    ws[own(b, 64), :] = sw[...]
    pl.semaphore_wait(barrier, len(near))

    def gather(full, rows):
        half = rows // 2

        def part(dy, dz, h):
            start = (at_y(dy) * 4 + at_zh(dz)) * rows + h * half
            return full.at[pl.ds(pl.multiple_of(start, 16), half), :]

        zcopy, ycopy = {}, {}

        def zsend_(dz_src, h, way):
            ref = part(0, dz_src, h)
            zcopy[(dz_src, h, way)] = single(ref, ref, device(y, at_zh(way), x, zl, c))

        def ysend_(dy_src, dz, h, way):
            ref = part(dy_src, dz, h)
            ycopy[(dy_src, dz, h, way)] = single(ref, ref, device(at_y(way), zh, x, zl, c))

        return zsend_, ysend_, zcopy, ycopy

    tz, ty, tzc, tyc = gather(wt, 96)
    sz, sy, szc, syc = gather(ws, 64)

    def y_both(ysend_, dz):
        for h in (0, 1):
            ysend_(0, dz, h, 1)
            ysend_(0, dz, h, 3)

    def y_forward(ysend_, yc, dz, h):
        if h == 0:
            yc[(0, dz, 0, 1)].wait_recv()
            ysend_(3, dz, 0, 1)
        else:
            yc[(0, dz, 1, 3)].wait_recv()
            ysend_(1, dz, 1, 3)

    tz(0, 0, 1)
    tz(0, 1, 3)
    tz(0, 1, 1)
    tz(0, 0, 3)
    slice_rows = pl.ds(pl.multiple_of((2 * x + c) * 64, 64), 64)
    swap = single(sf.at[slice_rows, :], sf2.at[slice_rows, :], device(at_y(2), zh, x, zl, c))
    y_both(ty, 0)

    def teacher_rows(i, carry):
        rows = pl.ds(pl.multiple_of(i * 128, 128), 128)
        wide = tf[rows, :].astype(F32)
        scale = lax.rsqrt(jnp.sum(wide * wide, axis=1, keepdims=True) + 1e-06)
        tu[rows, :] = (wide * scale).astype(BF16)
        return carry

    lax.fori_loop(0, 4, teacher_rows, 0)

    swap.wait_recv()
    s_feats = sem()
    for d in range(4):
        for e in range(2):
            if d or e:
                send(
                    sf2.at[slice_rows, :], sf2.at[slice_rows, :],
                    device(y, zh, at_x(d), zl, lax.rem(c + e, 2)), s_feats,
                )
    rest = sf2.at[pl.ds(0, 448), :]
    pending.append(lambda: wait_bytes(rest, ssem.at[s_feats]))

    y_forward(ty, tyc, 0, 0)
    y_forward(ty, tyc, 0, 1)
    tzc[(0, 0, 1)].wait_recv()
    tz(3, 0, 1)
    ty(0, 3, 0, 1)
    ty(0, 3, 0, 3)
    tzc[(0, 1, 3)].wait_recv()
    tz(1, 1, 3)
    ty(0, 1, 1, 1)
    ty(0, 1, 1, 3)
    sz(0, 0, 1)
    sz(0, 1, 3)
    sz(0, 1, 1)
    sz(0, 0, 3)
    y_forward(ty, tyc, 3, 0)
    y_forward(ty, tyc, 1, 1)
    tzc[(0, 1, 1)].wait_recv()
    ty(0, 3, 1, 1)
    ty(0, 3, 1, 3)
    tzc[(0, 0, 3)].wait_recv()
    ty(0, 1, 0, 1)
    ty(0, 1, 0, 3)
    y_forward(ty, tyc, 3, 1)
    y_forward(ty, tyc, 1, 0)
    tzc[(3, 0, 1)].wait_recv()
    ty(0, 2, 0, 1)
    ty(0, 2, 0, 3)
    tzc[(1, 1, 3)].wait_recv()
    ty(0, 2, 1, 1)
    ty(0, 2, 1, 3)
    y_both(sy, 0)

    wait_bytes(rest, rsem.at[s_feats])

    def student_rows(i, carry):
        rows = pl.ds(pl.multiple_of(i * 128, 128), 128)
        wide = sf2[rows, :].astype(F32)
        scale = lax.rsqrt(jnp.sum(wide * wide, axis=1, keepdims=True) + 1e-06)
        unit = wide * scale
        sh[rows, :] = unit.astype(BF16)
        sht[:, rows] = unit.T.astype(BF16)
        return carry

    lax.fori_loop(0, 4, student_rows, 0)

    y_forward(ty, tyc, 2, 0)
    y_forward(ty, tyc, 2, 1)
    for dz in (0, 3, 1, 2):
        tyc[(0, dz, 1, 1)].wait_recv()
        tyc[(0, dz, 0, 3)].wait_recv()
        tyc[(3, dz, 0, 1)].wait_recv()
        tyc[(1, dz, 1, 3)].wait_recv()

    def score_cols(j, carry):
        cols = pl.ds(pl.multiple_of(j * 256, 256), 256)
        scores = jnp.dot(tu[...], wt[:, cols], preferred_element_type=F32)
        block = jnp.exp(scores / TEACHER_TEMP)
        mass[:, cols] = block
        colmsg[0, :, cols] = jnp.sum(block, axis=0, keepdims=True)
        return carry

    lax.fori_loop(0, 4, score_cols, 0)

    def by_columns(factor, after):
        def body(i, carry):
            rows = pl.ds(pl.multiple_of(i * 64, 64), 64)
            part = jnp.zeros((64, 128), F32)
            for t in range(8):
                cols = slice(128 * t, 128 * t + 128)
                block = mass[rows, cols] * factor[:, cols]
                if after != 1.0:
                    block = block * after
                mass[rows, cols] = block
                part = part + block
            rowpart[rows, :] = part
            return carry

        lax.fori_loop(0, 8, body, 0)
        return lanes(rowpart[...])

    def by_rows(factor):
        rowb[...] = jnp.broadcast_to(factor, (128, ROWS)).T

        def body(i, carry):
            rows = pl.ds(pl.multiple_of(i * 64, 64), 64)
            by = rowb[rows, :]
            out = []
            for t in range(8):
                cols = slice(128 * t, 128 * t + 128)
                block = mass[rows, cols] * by
                mass[rows, cols] = block
                out.append(carry[t] + jnp.sum(block.reshape(8, 8, 128), axis=0))
            return tuple(out)

        sums = lax.fori_loop(0, 8, body, tuple(jnp.zeros((8, 128), F32) for _ in range(8)))
        return jnp.concatenate([jnp.sum(s, axis=0, keepdims=True) for s in sums], axis=1)

    def total_of(msg, buf):
        return msg + jnp.sum(buf[...], axis=0)

    def student_logits():
        def body(j, carry):
            cols = pl.ds(pl.multiple_of(j * 256, 256), 256)
            block = jnp.dot(sh[...], ws[:, cols], preferred_element_type=F32) / STUDENT_TEMP
            grown = jnp.exp(block)
            logit[:, cols] = block
            expo[:, cols] = grown
            part = grown[:, :128] + grown[:, 128:]
            totpart[...] = jnp.where(j == 0, part, totpart[...] + part)
            return carry

        lax.fori_loop(0, 4, body, 0)

    def student_near():
        szc[(0, 0, 1)].wait_recv()
        sz(3, 0, 1)
        szc[(0, 1, 3)].wait_recv()
        sz(1, 1, 3)
        for dz, h in ((3, 0), (1, 1)):
            sy(0, dz, h, 1)
            sy(0, dz, h, 3)
        y_forward(sy, syc, 0, 0)
        y_forward(sy, syc, 0, 1)
        szc[(0, 1, 1)].wait_recv()
        szc[(0, 0, 3)].wait_recv()
        for dz, h in ((3, 1), (1, 0)):
            sy(0, dz, h, 1)
            sy(0, dz, h, 3)

    def student_far():
        szc[(3, 0, 1)].wait_recv()
        szc[(1, 1, 3)].wait_recv()
        y_both(sy, 2)
        y_forward(sy, syc, 3, 0)
        y_forward(sy, syc, 1, 1)
        y_forward(sy, syc, 3, 1)
        y_forward(sy, syc, 1, 0)

    def student_last():
        y_forward(sy, syc, 2, 0)
        y_forward(sy, syc, 2, 1)

    def student_end():
        for dz in (0, 3, 1, 2):
            syc[(0, dz, 1, 1)].wait_recv()
            syc[(0, dz, 0, 3)].wait_recv()
            syc[(3, dz, 0, 1)].wait_recv()
            syc[(1, dz, 1, 3)].wait_recv()
        student_logits()

    for step in range(3):
        got = batch_send(colmsg.at[step], colbuf.at[step])
        if step == 0:
            student_near()
        if step == 1:
            student_last()
        if step == 2:
            student_end()
            lastmsg[:, 512:] = lanes(totpart[...])
        got()
        col_total = total_of(colmsg[step], colbuf.at[step]) * PROTOS
        if step == 0:
            factor = 1.0 / (col_total * 0.25)
            row_sum = by_columns(factor, 0.25)
        else:
            row_sum = by_columns(1.0 / col_total, 1.0)
        if step < 2:
            rowmsg[step] = row_sum
            got = proto_send(rowmsg.at[step], rowbuf.at[step])
            if step == 0:
                student_far()
            got()
            row_total = total_of(rowmsg[step], rowbuf.at[step])
            colmsg[step + 1] = by_rows(1.0 / (CROPS * row_total))
        else:
            lastmsg[:, :512] = row_sum
            got = proto_send(lastmsg, lastbuf)
            got()
    both = total_of(lastmsg[...], lastbuf)
    row_total, total = both[:, :512], both[:, 512:]
    target_factor = CROPS * (1.0 / (CROPS * row_total))
    weight_sum = target_factor * row_total
    rowb[...] = jnp.broadcast_to(target_factor, (128, ROWS)).T
    probb[...] = jnp.broadcast_to(weight_sum * inverse(total, GAIN), (128, ROWS)).T
    crop_term = jnp.sum(weight_sum * jnp.log(total), axis=1, keepdims=True) / 32.0

    def slope_rows(i, carry):
        rows = pl.ds(pl.multiple_of(i * 64, 64), 64)
        by, prob = rowb[rows, :], probb[rows, :]
        for t in range(8):
            cols = slice(128 * t, 128 * t + 128)
            target = mass[rows, cols] * by
            slope[rows, cols] = (expo[rows, cols] * prob - target * GAIN).astype(BF16)
            carry = carry + jnp.sum((target * logit[rows, cols]).reshape(8, 8, 128), axis=0)
        return carry

    pairs = lax.fori_loop(0, 8, slope_rows, jnp.zeros((8, 128), F32))
    pairs = jnp.sum(jnp.sum(pairs, axis=0, keepdims=True), axis=1, keepdims=True)
    lossmsg[0] = jnp.broadcast_to(crop_term - pairs, (1, 128))

    def back_half(half, store):
        rows = pl.ds(pl.multiple_of(half * 256, 256), 256)

        def body(j, carry):
            feats = pl.ds(pl.multiple_of(j * 256, 256), 256)
            store(feats, nt(slope[rows, :], ws[feats, :]))
            return carry

        lax.fori_loop(0, 4, body, 0)

    def store_send(feats, value):
        bsend[:, feats] = value.astype(BF16)

    def store_own(feats, value):
        bown[:, feats] = value

    back_half(1 - c, store_send)
    core_copy = single(bsend, brecv, device(y, zh, x, zl, 1 - c))

    ycopies = []
    for q in range(4):
        cols = slice(256 * q, 256 * q + 256)
        copies = []
        for dy in (2, 1, 3, 0):
            rows = pl.ds(pl.multiple_of(at_y(dy) * 256, 256), 256)
            value = jnp.dot(sht[rows, :], slope[:, cols], preferred_element_type=F32)
            if dy:
                gsend[q, dy - 1] = value.astype(BF16)
                copies.append(
                    single(gsend.at[q, dy - 1], grecv.at[q, dy - 1], device(at_y(dy), zh, x, zl, c))
                )
            else:
                gown[q] = value
        ycopies.append(copies)
        if q == 0:
            back_half(c, store_own)

    loss_got = proto_send(lossmsg.at[0], lossrow)

    core_copy.wait_recv()
    xcopies = []
    for d in (2, 1, 3):
        rows = pl.ds(pl.multiple_of(at_x(d) * 64, 64), 64)
        xsend[d - 1] = (bown[rows, :] + brecv[rows, :].astype(F32)).astype(BF16)
        xcopies.append(single(xsend.at[d - 1], xrecv.at[d - 1], device(y, zh, at_x(d), zl, c)))

    zcopies = []

    def weight_z(q):
        for copy in ycopies[q]:
            copy.wait_recv()
        copies = []
        for dz in (2, 1, 3, 0):
            rows = pl.ds(pl.multiple_of(at_zh(dz) * 64, 64), 64)
            value = gown[q, rows, :]
            for d in range(3):
                value = value + grecv[q, d, rows, :].astype(F32)
            if dz:
                zsend[q, dz - 1] = value.astype(BF16)
                copies.append(
                    single(zsend.at[q, dz - 1], zrecv.at[q, dz - 1], device(y, at_zh(dz), x, zl, c))
                )
            else:
                zown[q] = value
        zcopies.append(copies)

    weight_z(0)

    for copy in xcopies:
        copy.wait_recv()
    rows = pl.ds(pl.multiple_of(x * 64, 64), 64)
    xsum = bown[rows, :] + brecv[rows, :].astype(F32)
    for d in range(3):
        xsum = xsum + xrecv[d].astype(F32)
    bown[pl.ds(0, 64), :] = xsum
    lcopies = []
    for d in (2, 1, 3):
        fl = lax.rem(zl + d, 4)
        rows = pl.ds(pl.multiple_of(fl * 16, 16), 16)
        lsend[d - 1] = bown[rows, :].astype(BF16)
        lcopies.append(single(lsend.at[d - 1], lrecv.at[d - 1], device(y, zh, x, fl, c)))

    weight_z(1)
    loss_got()
    lossmsg[1] = lossmsg[0] + jnp.sum(lossrow[...], axis=0)
    loss_got = batch_send(lossmsg.at[1], losscol)

    for copy in lcopies:
        copy.wait_recv()
    rows = pl.ds(pl.multiple_of(zl * 16, 16), 16)
    back = bown[rows, :]
    for d in range(3):
        back = back + lrecv[d].astype(F32)
    mine = pl.ds(pl.multiple_of(c * 256 + x * 64 + zl * 16, 16), 16)
    wide = sf2[mine, :].astype(F32)
    scale = lax.rsqrt(jnp.sum(wide * wide, axis=1, keepdims=True) + 1e-06)
    unit = wide * scale
    inner = jnp.sum(unit * back, axis=1, keepdims=True)
    gfin[...] = ((back - unit * inner) * scale).astype(BF16)
    fcopies = []
    for d in range(4):
        fl = lax.rem(zl + d, 4)
        fcopies.append(single(gfin, gfs.at[mine, :], device(at_y(2), zh, x, fl, c)))

    weight_z(2)

    for copy in fcopies:
        copy.wait_recv()

    def piece(dx, core):
        return gfs.at[pl.ds(pl.multiple_of(core * 256 + at_x(dx) * 64, 64), 64), :]

    lastx = []
    for d in (2, 1, 3):
        lastx.append(single(piece(0, c), piece(0, c), device(y, zh, at_x(d), zl, c)))
    lastc = [single(piece(0, c), piece(0, c), device(y, zh, x, zl, 1 - c))]

    weight_z(3)

    for d, copy in zip((2, 1, 3), lastx):
        copy.wait_recv()
        lastc.append(single(piece(4 - d, c), piece(4 - d, c), device(y, zh, x, zl, 1 - c)))

    for q in range(4):
        cols = slice(256 * q, 256 * q + 256)
        for copy in zcopies[q]:
            copy.wait_recv()
        value = zown[q]
        for d in range(3):
            value = value + zrecv[q, d].astype(F32)
        gw_out[:, cols] = value.astype(BF16)

    loss_got()
    loss_out[...] = (lossmsg[1] + jnp.sum(losscol[...], axis=0)) / CROPS

    for copy in lastc:
        copy.wait_recv()
    gf_out[...] = gfs[...]
    for done in pending:
        done()


def shards(teacher_feats, teacher_weight, student_feats, student_weight):
    vm = pltpu.VMEM
    spec = pl.BlockSpec(memory_space=pltpu.VMEM)
    loss, grad_weight, grad_feats = pl.pallas_call(
        kernel,
        out_shape=(
            jax.ShapeDtypeStruct((1, 128), F32),
            jax.ShapeDtypeStruct((64, COLS), BF16),
            jax.ShapeDtypeStruct((ROWS, DS), BF16),
        ),
        in_specs=[spec] * 4,
        out_specs=(spec,) * 3,
        scratch_shapes=[
            vm((ROWS, DT), BF16),
            vm((DT, COLS), BF16),
            vm((DS, COLS), BF16),
            vm((ROWS, DS), BF16),
            vm((ROWS, DS), BF16),
            vm((DS, ROWS), BF16),
            vm((ROWS, COLS), F32),
            vm((ROWS, COLS), F32),
            vm((ROWS, COLS), F32),
            vm((ROWS, COLS), BF16),
            vm((ROWS, 128), F32),
            vm((ROWS, 128), F32),
            vm((ROWS, 128), F32),
            vm((ROWS, 128), F32),
            vm((3, 1, COLS), F32),
            vm((3, 15, 1, COLS), F32),
            vm((2, 1, ROWS), F32),
            vm((2, 31, 1, ROWS), F32),
            vm((1, 2 * ROWS), F32),
            vm((31, 1, 2 * ROWS), F32),
            vm((2, 1, 128), F32),
            vm((31, 1, 128), F32),
            vm((15, 1, 128), F32),
            vm((256, DS), BF16),
            vm((256, DS), F32),
            vm((256, DS), BF16),
            vm((3, 64, DS), BF16),
            vm((3, 64, DS), BF16),
            vm((3, 16, DS), BF16),
            vm((3, 16, DS), BF16),
            vm((16, DS), BF16),
            vm((ROWS, DS), BF16),
            vm((4, 3, 256, 256), BF16),
            vm((4, 256, 256), F32),
            vm((4, 3, 256, 256), BF16),
            vm((4, 3, 64, 256), BF16),
            vm((4, 64, 256), F32),
            vm((4, 3, 64, 256), BF16),
            pltpu.SemaphoreType.DMA((NSEM,)),
            pltpu.SemaphoreType.DMA((NSEM,)),
        ],
        compiler_params=pltpu.CompilerParams(
            collective_id=0, has_side_effects=True, vmem_limit_bytes=56 * 2**20
        ),
    )(teacher_feats, teacher_weight, student_feats, student_weight)
    return (loss[0, 0], grad_weight, grad_feats)


def solution(mesh):
    return jax.shard_map(
        shards,
        mesh=mesh,
        in_specs=(P("batch", None), P("batch", "proto"), P("batch", None), P("batch", "proto")),
        out_specs=(P(), P("batch", "proto"), P("batch", None)),
        check_vma=False,
    )
```

```python
import jax
import jax.numpy as jnp
from jax import lax
from jax.experimental import pallas as pl
from jax.experimental.pallas import tpu as pltpu
from jax.sharding import PartitionSpec as P

F32 = jnp.float32
BF16 = jnp.bfloat16
MESH = pl.DeviceIdType.MESH

TEACHER_TEMP = 0.07
STUDENT_TEMP = 0.1
LOSS_SCALE = 1024.0
CROPS = 8192.0
PROTOS = 32768.0
GAIN = LOSS_SCALE / STUDENT_TEMP

ROWS = 512
COLS = 1024
DT = 1536
DS = 1024
NSEM = 256
TPIECE = 1024


def device(y, zh, x, zl, c):
    return (y * 4 + zh, (x * 4 + zl) * 2 + c)


def nt(a, b):
    return lax.dot_general(a, b, (((1,), (1,)), ((), ())), preferred_element_type=F32)


def lanes(part):
    ones = jnp.ones((8, 128), F32)
    out = lax.dot_general(
        ones, part, (((1,), (1,)), ((), ())),
        precision=lax.Precision.HIGHEST, preferred_element_type=F32,
    )
    return out[0:1, :]


def inverse(value, gain):
    part = jnp.where(value > 1.0, 0.25, 1.0)
    return (1.0 / (value * part)) * (part * gain)


def kernel(
    tf, tw, sf, sw, loss_out, gw_out, gf_out,
    tu, wt, ws, sf2, sh, sht, mass, logit, expo, slope,
    rowpart, totpart, rowb, probb,
    colmsg, colbuf, rowmsg, rowbuf, lastmsg, lastbuf,
    lossmsg, lossrow, losscol,
    bsend, bown, brecv, xsend, xrecv, lsend, lrecv, gfin, gfs,
    gsend, gkeep, gown, grecv, zsend, zrecv,
    ssem, rsem,
):
    b = lax.axis_index("batch")
    p = lax.axis_index("proto")
    y, zh = b // 4, b % 4
    x, zl, c = p // 8, (p // 2) % 4, p % 2

    def at_y(d):
        return lax.rem(y + d, 4)

    def at_zh(d):
        return lax.rem(zh + d, 4)

    def at_x(d):
        return lax.rem(x + d, 4)

    used = [0]
    pending = []

    def sem():
        used[0] += 1
        return used[0] - 1

    def send(src, dst, dev, s=None, r=None):
        s = sem() if s is None else s
        r = s if r is None else r
        copy = pltpu.make_async_remote_copy(
            src_ref=src, dst_ref=dst, send_sem=ssem.at[s], recv_sem=rsem.at[r],
            device_id=dev, device_id_type=MESH,
        )
        copy.start()
        return copy

    def single(src, dst, dev):
        copy = send(src, dst, dev)
        pending.append(copy.wait_send)
        return copy

    def wait_bytes(ref, s):
        pltpu.make_async_copy(ref, ref, s).wait()

    def batch_send(src, buf):
        s = sem()
        for dz in (2, 1, 3, 0):
            for dy in (2, 1, 3, 0):
                if dy or dz:
                    send(src, buf.at[dy * 4 + dz - 1], device(at_y(dy), at_zh(dz), x, zl, c), s)
        pending.append(lambda: wait_bytes(buf, ssem.at[s]))
        return lambda: wait_bytes(buf, rsem.at[s])

    def proto_send(src, buf):
        s = sem()

        def body(i, carry):
            k = 31 - i
            dx, dl, dc = k // 8, (k // 2) % 4, k % 2
            fl = lax.rem(zl + dl, 4)
            send(src, buf.at[k - 1], device(y, zh, at_x(dx), fl, lax.rem(c + dc, 2)), s)
            return carry

        lax.fori_loop(0, 31, body, 0)
        pending.append(lambda: wait_bytes(buf, ssem.at[s]))
        return lambda: wait_bytes(buf, rsem.at[s])

    near = [device(at_y(d), zh, x, zl, c) for d in (1, 2, 3)]
    near += [device(y, at_zh(d), x, zl, c) for d in (1, 2, 3)]
    near += [device(y, zh, x, lax.rem(zl + d, 4), c) for d in (1, 2, 3)]
    near += [
        device(y, zh, at_x(d), zl, lax.rem(c + e, 2))
        for d in range(4) for e in range(2) if d or e
    ]
    barrier = pltpu.get_barrier_semaphore()
    for dev in near:
        pl.semaphore_signal(barrier, inc=1, device_id=dev, device_id_type=MESH)

    def own(block, size):
        return pl.ds(pl.multiple_of(block * size, 16), size)

    wt[own(b, 96), :] = tw[...]
    ws[own(b, 64), :] = sw[...]
    pl.semaphore_wait(barrier, len(near))
    def gather(full, rows, width):
        half = rows // 2

        def part(dy, dz, h, k):
            start = (at_y(dy) * 4 + at_zh(dz)) * rows + h * half
            return full.at[pl.ds(pl.multiple_of(start, 16), half), pl.ds(k * width, width)]

        zc, yc = {}, {}
        ks = range(COLS // width)

        def zs(dz, h, way, k):
            ref = part(0, dz, h, k)
            zc[dz, h, way, k] = single(ref, ref, device(y, at_zh(way), x, zl, c))

        def ys(dy, dz, h, way, k):
            ref = part(dy, dz, h, k)
            yc[dy, dz, h, way, k] = single(ref, ref, device(at_y(way), zh, x, zl, c))

        def start():
            for way, h in ((1, 0), (3, 1), (1, 1), (3, 0)):
                for k in ks:
                    zs(0, h, way, k)

        def both(dz, h, k):
            ys(0, dz, h, 1, k)
            ys(0, dz, h, 3, k)

        def forward(dz, h, k):
            way, source = ((1, 3), (3, 1))[h]
            yc[0, dz, h, way, k].wait_recv()
            ys(source, dz, h, way, k)

        def first(h, k):
            way, source = ((1, 3), (3, 1))[h]
            zc[0, h, way, k].wait_recv()
            both(source, h, k)
            zs(source, h, way, k)

        def second(h, k):
            way, source = ((3, 1), (1, 3))[h]
            zc[0, h, way, k].wait_recv()
            both(source, h, k)

        def third(h, k):
            way, source = ((1, 3), (3, 1))[h]
            zc[source, h, way, k].wait_recv()
            both(2, h, k)

        def finish():
            for dz in (0, 3, 1, 2):
                for k in ks:
                    yc[0, dz, 1, 1, k].wait_recv()
                    yc[0, dz, 0, 3, k].wait_recv()
                    yc[3, dz, 0, 1, k].wait_recv()
                    yc[1, dz, 1, 3, k].wait_recv()

        return start, both, forward, first, second, third, finish

    t_start, t_both, t_forward, t_first, t_second, t_third, t_finish = gather(wt, 96, TPIECE)
    s_start, s_both, s_forward, s_first, s_second, s_third, s_finish = gather(ws, 64, COLS)
    tks = range(COLS // TPIECE)

    for k in tks:
        t_both(0, 0, k)
        t_both(0, 1, k)
    t_start()
    slice_rows = pl.ds(pl.multiple_of((2 * x + c) * 64, 64), 64)
    swap = single(sf.at[slice_rows, :], sf2.at[slice_rows, :], device(at_y(2), zh, x, zl, c))

    def teacher_rows(i, carry):
        rows = pl.ds(pl.multiple_of(i * 128, 128), 128)
        wide = tf[rows, :].astype(F32)
        scale = lax.rsqrt(jnp.sum(wide * wide, axis=1, keepdims=True) + 1e-06)
        tu[rows, :] = (wide * scale).astype(BF16)
        return carry

    lax.fori_loop(0, 4, teacher_rows, 0)

    swap.wait_recv()
    s_feats = sem()
    for d in range(4):
        for e in range(2):
            if d or e:
                send(
                    sf2.at[slice_rows, :], sf2.at[slice_rows, :],
                    device(y, zh, at_x(d), zl, lax.rem(c + e, 2)), s_feats,
                )
    rest = sf2.at[pl.ds(0, 448), :]
    pending.append(lambda: wait_bytes(rest, ssem.at[s_feats]))

    for k in tks:
        t_forward(0, 0, k)
        t_forward(0, 1, k)
    for k in tks:
        t_first(0, k)
        t_first(1, k)
    for k in tks:
        t_forward(3, 0, k)
        t_forward(1, 1, k)
    for k in tks:
        t_second(1, k)
        t_second(0, k)
    for k in tks:
        t_third(0, k)
        t_third(1, k)
        t_forward(3, 1, k)
        t_forward(1, 0, k)
    s_start()
    for k in tks:
        t_forward(2, 0, k)
        t_forward(2, 1, k)
    t_finish()
    def score_cols(j, carry):
        cols = pl.ds(pl.multiple_of(j * 256, 256), 256)
        scores = jnp.dot(tu[...], wt[:, cols], preferred_element_type=F32)
        block = jnp.exp(scores / TEACHER_TEMP)
        mass[:, cols] = block
        colmsg[0, :, cols] = jnp.sum(block, axis=0, keepdims=True)
        return carry

    lax.fori_loop(0, 4, score_cols, 0)

    def by_columns(factor, after):
        def body(i, carry):
            rows = pl.ds(pl.multiple_of(i * 64, 64), 64)
            part = jnp.zeros((64, 128), F32)
            for t in range(8):
                cols = slice(128 * t, 128 * t + 128)
                block = mass[rows, cols] * factor[:, cols]
                if after != 1.0:
                    block = block * after
                mass[rows, cols] = block
                part = part + block
            rowpart[rows, :] = part
            return carry

        lax.fori_loop(0, 8, body, 0)
        return lanes(rowpart[...])

    def by_rows(factor):
        rowb[...] = jnp.broadcast_to(factor, (128, ROWS)).T

        def body(i, carry):
            rows = pl.ds(pl.multiple_of(i * 64, 64), 64)
            by = rowb[rows, :]
            out = []
            for t in range(8):
                cols = slice(128 * t, 128 * t + 128)
                block = mass[rows, cols] * by
                mass[rows, cols] = block
                out.append(carry[t] + jnp.sum(block.reshape(8, 8, 128), axis=0))
            return tuple(out)

        sums = lax.fori_loop(0, 8, body, tuple(jnp.zeros((8, 128), F32) for _ in range(8)))
        return jnp.concatenate([jnp.sum(s, axis=0, keepdims=True) for s in sums], axis=1)

    def total_of(msg, buf):
        return msg + jnp.sum(buf[...], axis=0)

    def student_rows(i, carry):
        rows = pl.ds(pl.multiple_of(i * 128, 128), 128)
        wide = sf2[rows, :].astype(F32)
        scale = lax.rsqrt(jnp.sum(wide * wide, axis=1, keepdims=True) + 1e-06)
        unit = wide * scale
        sh[rows, :] = unit.astype(BF16)
        sht[:, rows] = unit.T.astype(BF16)
        return carry

    def student_logits():
        def body(j, carry):
            cols = pl.ds(pl.multiple_of(j * 256, 256), 256)
            block = jnp.dot(sh[...], ws[:, cols], preferred_element_type=F32) / STUDENT_TEMP
            grown = jnp.exp(block)
            logit[:, cols] = block
            expo[:, cols] = grown
            part = grown[:, :128] + grown[:, 128:]
            totpart[...] = jnp.where(j == 0, part, totpart[...] + part)
            return carry

        lax.fori_loop(0, 4, body, 0)

    def student_near():
        s_first(0, 0)
        s_first(1, 0)
        s_forward(0, 0, 0)
        s_forward(0, 1, 0)
        s_second(1, 0)
        s_second(0, 0)

    def student_far():
        s_third(0, 0)
        s_third(1, 0)
        s_forward(3, 0, 0)
        s_forward(1, 1, 0)
        s_forward(3, 1, 0)
        s_forward(1, 0, 0)

    def student_last():
        s_forward(2, 0, 0)
        s_forward(2, 1, 0)

    def student_end():
        s_finish()
        student_logits()
    for step in range(3):
        got = batch_send(colmsg.at[step], colbuf.at[step])
        if step == 0:
            s_both(0, 0, 0)
            s_both(0, 1, 0)
            wait_bytes(rest, rsem.at[s_feats])
            lax.fori_loop(0, 4, student_rows, 0)
            student_near()
        if step == 1:
            student_far()
        if step == 2:
            student_end()
            lastmsg[:, 512:] = lanes(totpart[...])
        got()
        col_total = total_of(colmsg[step], colbuf.at[step]) * PROTOS
        if step == 0:
            factor = 1.0 / (col_total * 0.25)
            row_sum = by_columns(factor, 0.25)
        else:
            row_sum = by_columns(1.0 / col_total, 1.0)
        if step < 2:
            rowmsg[step] = row_sum
            got = proto_send(rowmsg.at[step], rowbuf.at[step])
            if step == 1:
                student_last()
            got()
            row_total = total_of(rowmsg[step], rowbuf.at[step])
            colmsg[step + 1] = by_rows(1.0 / (CROPS * row_total))
        else:
            lastmsg[:, :512] = row_sum
            got = proto_send(lastmsg, lastbuf)
            got()
    both = total_of(lastmsg[...], lastbuf)
    row_total, total = both[:, :512], both[:, 512:]
    target_factor = CROPS * (1.0 / (CROPS * row_total))
    weight_sum = target_factor * row_total
    rowb[...] = jnp.broadcast_to(target_factor, (128, ROWS)).T
    probb[...] = jnp.broadcast_to(weight_sum * inverse(total, GAIN), (128, ROWS)).T
    crop_term = jnp.sum(weight_sum * jnp.log(total), axis=1, keepdims=True) / 32.0
    def slope_rows(i, carry):
        rows = pl.ds(pl.multiple_of(i * 64, 64), 64)
        by, prob = rowb[rows, :], probb[rows, :]
        for t in range(8):
            cols = slice(128 * t, 128 * t + 128)
            target = mass[rows, cols] * by
            slope[rows, cols] = (expo[rows, cols] * prob - target * GAIN).astype(BF16)
            carry = carry + jnp.sum((target * logit[rows, cols]).reshape(8, 8, 128), axis=0)
        return carry

    pairs = lax.fori_loop(0, 8, slope_rows, jnp.zeros((8, 128), F32))
    pairs = jnp.sum(jnp.sum(pairs, axis=0, keepdims=True), axis=1, keepdims=True)
    lossmsg[0] = jnp.broadcast_to(crop_term - pairs, (1, 128))
    def back_half(half, store):
        rows = pl.ds(pl.multiple_of(half * 256, 256), 256)

        def body(j, carry):
            feats = pl.ds(pl.multiple_of(j * 256, 256), 256)
            store(feats, nt(slope[rows, :], ws[feats, :]))
            return carry

        lax.fori_loop(0, 4, body, 0)

    def store_send(feats, value):
        bsend[:, feats] = value.astype(BF16)

    def store_own(feats, value):
        bown[:, feats] = value

    back_half(1 - c, store_send)
    core_copy = single(bsend, brecv, device(y, zh, x, zl, 1 - c))

    up, down = device(at_y(1), zh, x, zl, c), device(at_y(3), zh, x, zl, c)
    ysent, yfwd, zcopies = {}, {}, []

    def weight_made(q):
        cols = slice(256 * q, 256 * q + 256)
        for dy in (2, 1, 3, 0):
            rows = pl.ds(pl.multiple_of(at_y(dy) * 256, 256), 256)
            value = jnp.dot(sht[rows, :], slope[:, cols], preferred_element_type=F32)
            if dy == 2:
                gsend[q, 0] = value[:128].astype(BF16)
                gsend[q, 1] = value[128:].astype(BF16)
            elif dy == 1:
                gkeep[q, 0] = value[:128]
                gsend[q, 2] = value[128:].astype(BF16)
            elif dy == 3:
                gsend[q, 3] = value[:128].astype(BF16)
                gkeep[q, 1] = value[128:]
            else:
                gown[q] = value

    def weight_send(q):
        ysent[q] = [
            single(gsend.at[q, i], grecv.at[q, i], (up, down)[i % 2]) for i in range(4)
        ]

    def weight_forward(q):
        for i in range(2):
            ysent[q][i].wait_recv()
            gsend[q, 4 + i] = (gkeep[q, i] + grecv[q, i].astype(F32)).astype(BF16)
            yfwd[q, i] = single(gsend.at[q, 4 + i], grecv.at[q, 4 + i], (up, down)[i])

    weight_made(0)
    weight_send(0)
    back_half(c, store_own)
    weight_made(1)
    loss_got = proto_send(lossmsg.at[0], lossrow)

    core_copy.wait_recv()
    xcopies = []
    for d in (2, 1, 3):
        rows = pl.ds(pl.multiple_of(at_x(d) * 64, 64), 64)
        xsend[d - 1] = (bown[rows, :] + brecv[rows, :].astype(F32)).astype(BF16)
        xcopies.append(single(xsend.at[d - 1], xrecv.at[d - 1], device(y, zh, at_x(d), zl, c)))

    def weight_z(q):
        ysent[q][2].wait_recv()
        ysent[q][3].wait_recv()
        yfwd[q, 0].wait_recv()
        yfwd[q, 1].wait_recv()
        low = gown[q, :128] + grecv[q, 3].astype(F32) + grecv[q, 4].astype(F32)
        high = gown[q, 128:] + grecv[q, 2].astype(F32) + grecv[q, 5].astype(F32)
        gown[q, :128] = low
        gown[q, 128:] = high
        copies = []
        for dz in (2, 1, 3):
            rows = pl.ds(pl.multiple_of(at_zh(dz) * 64, 64), 64)
            zsend[q, dz - 1] = gown[q, rows, :].astype(BF16)
            copies.append(
                single(zsend.at[q, dz - 1], zrecv.at[q, dz - 1], device(y, at_zh(dz), x, zl, c))
            )
        zcopies.append(copies)

    weight_forward(0)
    weight_send(1)
    weight_made(2)
    weight_z(0)
    weight_forward(1)
    weight_send(2)
    weight_made(3)

    for copy in xcopies:
        copy.wait_recv()
    rows = pl.ds(pl.multiple_of(x * 64, 64), 64)
    xsum = bown[rows, :] + brecv[rows, :].astype(F32)
    for d in range(3):
        xsum = xsum + xrecv[d].astype(F32)
    bown[pl.ds(0, 64), :] = xsum
    lcopies = []
    for d in (2, 1, 3):
        fl = lax.rem(zl + d, 4)
        rows = pl.ds(pl.multiple_of(fl * 16, 16), 16)
        lsend[d - 1] = bown[rows, :].astype(BF16)
        lcopies.append(single(lsend.at[d - 1], lrecv.at[d - 1], device(y, zh, x, fl, c)))
    weight_z(1)
    weight_forward(2)
    weight_send(3)
    loss_got()
    lossmsg[1] = lossmsg[0] + jnp.sum(lossrow[...], axis=0)
    loss_got = batch_send(lossmsg.at[1], losscol)

    for copy in lcopies:
        copy.wait_recv()
    rows = pl.ds(pl.multiple_of(zl * 16, 16), 16)
    back = bown[rows, :]
    for d in range(3):
        back = back + lrecv[d].astype(F32)
    mine = pl.ds(pl.multiple_of(c * 256 + x * 64 + zl * 16, 16), 16)
    wide = sf2[mine, :].astype(F32)
    scale = lax.rsqrt(jnp.sum(wide * wide, axis=1, keepdims=True) + 1e-06)
    unit = wide * scale
    inner = jnp.sum(unit * back, axis=1, keepdims=True)
    gfin[...] = ((back - unit * inner) * scale).astype(BF16)
    fcopies = []
    for d in range(4):
        fl = lax.rem(zl + d, 4)
        fcopies.append(single(gfin, gfs.at[mine, :], device(at_y(2), zh, x, fl, c)))
    weight_z(2)
    weight_forward(3)

    for copy in fcopies:
        copy.wait_recv()

    def piece(dx, core):
        return gfs.at[pl.ds(pl.multiple_of(core * 256 + at_x(dx) * 64, 64), 64), :]

    lastx = []
    for d in (2, 1, 3):
        lastx.append(single(piece(0, c), piece(0, c), device(y, zh, at_x(d), zl, c)))
    lastc = [single(piece(0, c), piece(0, c), device(y, zh, x, zl, 1 - c))]
    weight_z(3)

    for d, copy in zip((2, 1, 3), lastx):
        copy.wait_recv()
        lastc.append(single(piece(4 - d, c), piece(4 - d, c), device(y, zh, x, zl, 1 - c)))

    for q in range(4):
        cols = slice(256 * q, 256 * q + 256)
        for copy in zcopies[q]:
            copy.wait_recv()
        value = gown[q, pl.ds(pl.multiple_of(zh * 64, 64), 64), :]
        for d in range(3):
            value = value + zrecv[q, d].astype(F32)
        gw_out[:, cols] = value.astype(BF16)
    loss_got()
    loss_out[...] = (lossmsg[1] + jnp.sum(losscol[...], axis=0)) / CROPS

    for copy in lastc:
        copy.wait_recv()
    gf_out[...] = gfs[...]
    for done in pending:
        done()


def shards(teacher_feats, teacher_weight, student_feats, student_weight):
    vm = pltpu.VMEM
    spec = pl.BlockSpec(memory_space=pltpu.VMEM)
    loss, grad_weight, grad_feats = pl.pallas_call(
        kernel,
        out_shape=(
            jax.ShapeDtypeStruct((1, 128), F32),
            jax.ShapeDtypeStruct((64, COLS), BF16),
            jax.ShapeDtypeStruct((ROWS, DS), BF16),
        ),
        in_specs=[spec] * 4,
        out_specs=(spec,) * 3,
        scratch_shapes=[
            vm((ROWS, DT), BF16),
            vm((DT, COLS), BF16),
            vm((DS, COLS), BF16),
            vm((ROWS, DS), BF16),
            vm((ROWS, DS), BF16),
            vm((DS, ROWS), BF16),
            vm((ROWS, COLS), F32),
            vm((ROWS, COLS), F32),
            vm((ROWS, COLS), F32),
            vm((ROWS, COLS), BF16),
            vm((ROWS, 128), F32),
            vm((ROWS, 128), F32),
            vm((ROWS, 128), F32),
            vm((ROWS, 128), F32),
            vm((3, 1, COLS), F32),
            vm((3, 15, 1, COLS), F32),
            vm((2, 1, ROWS), F32),
            vm((2, 31, 1, ROWS), F32),
            vm((1, 2 * ROWS), F32),
            vm((31, 1, 2 * ROWS), F32),
            vm((2, 1, 128), F32),
            vm((31, 1, 128), F32),
            vm((15, 1, 128), F32),
            vm((256, DS), BF16),
            vm((256, DS), F32),
            vm((256, DS), BF16),
            vm((3, 64, DS), BF16),
            vm((3, 64, DS), BF16),
            vm((3, 16, DS), BF16),
            vm((3, 16, DS), BF16),
            vm((16, DS), BF16),
            vm((ROWS, DS), BF16),
            vm((4, 6, 128, 256), BF16),
            vm((4, 2, 128, 256), F32),
            vm((4, 256, 256), F32),
            vm((4, 6, 128, 256), BF16),
            vm((4, 3, 64, 256), BF16),
            vm((4, 3, 64, 256), BF16),
            pltpu.SemaphoreType.DMA((NSEM,)),
            pltpu.SemaphoreType.DMA((NSEM,)),
        ],
        compiler_params=pltpu.CompilerParams(
            collective_id=0, has_side_effects=True, vmem_limit_bytes=56 * 2**20
        ),
    )(teacher_feats, teacher_weight, student_feats, student_weight)
    return (loss[0, 0], grad_weight, grad_feats)


def solution(mesh):
    return jax.shard_map(
        shards,
        mesh=mesh,
        in_specs=(P("batch", None), P("batch", "proto"), P("batch", None), P("batch", "proto")),
        out_specs=(P(), P("batch", "proto"), P("batch", None)),
        check_vma=False,
    )
```

```python
import jax
import jax.numpy as jnp
from jax import lax
from jax.experimental import pallas as pl
from jax.experimental.pallas import tpu as pltpu
from jax.sharding import PartitionSpec as P

F32 = jnp.float32
BF16 = jnp.bfloat16
MESH = pl.DeviceIdType.MESH

TEACHER_TEMP = 0.07
STUDENT_TEMP = 0.1
LOSS_SCALE = 1024.0
CROPS = 8192.0
PROTOS = 32768.0
GAIN = LOSS_SCALE / STUDENT_TEMP

ROWS = 512
COLS = 1024
DT = 1536
DS = 1024
NSEM = 256
TPIECE = 1024


def device(y, zh, x, zl, c):
    return (y * 4 + zh, (x * 4 + zl) * 2 + c)


def nt(a, b):
    return lax.dot_general(a, b, (((1,), (1,)), ((), ())), preferred_element_type=F32)


def lanes(part):
    ones = jnp.ones((8, 128), F32)
    out = lax.dot_general(
        ones, part, (((1,), (1,)), ((), ())),
        precision=lax.Precision.HIGHEST, preferred_element_type=F32,
    )
    return out[0:1, :]


def inverse(value, gain):
    part = jnp.where(value > 1.0, 0.25, 1.0)
    return (1.0 / (value * part)) * (part * gain)


def kernel(
    tf_in, tw, sf, sw, loss_out, gw_out, gf_out,
    tf,
    tu, wt, ws, sf2, sh, sht, mass, logit, expo, slope,
    rowpart, totpart, rowb, probb,
    colmsg, colbuf, rowmsg, rowbuf, lastmsg, lastbuf,
    lossmsg, lossrow, losscol,
    bsend, bown, brecv, xsend, xrecv, lsend, lrecv, gfin, gfs,
    gsend, gkeep, gown, grecv, zsend, zrecv,
    ssem, rsem, isem,
):
    b = lax.axis_index("batch")
    p = lax.axis_index("proto")
    y, zh = b // 4, b % 4
    x, zl, c = p // 8, (p // 2) % 4, p % 2

    def at_y(d):
        return lax.rem(y + d, 4)

    def at_zh(d):
        return lax.rem(zh + d, 4)

    def at_x(d):
        return lax.rem(x + d, 4)

    fetch = pltpu.make_async_copy(tf_in, tf, isem)
    fetch.start()

    used = [0]
    pending = []

    def sem():
        used[0] += 1
        return used[0] - 1

    def send(src, dst, dev, s=None, r=None):
        s = sem() if s is None else s
        r = s if r is None else r
        copy = pltpu.make_async_remote_copy(
            src_ref=src, dst_ref=dst, send_sem=ssem.at[s], recv_sem=rsem.at[r],
            device_id=dev, device_id_type=MESH,
        )
        copy.start()
        return copy

    def single(src, dst, dev):
        copy = send(src, dst, dev)
        pending.append(copy.wait_send)
        return copy

    def wait_bytes(ref, s):
        pltpu.make_async_copy(ref, ref, s).wait()

    def batch_send(src, buf):
        s = sem()
        for dz in (2, 1, 3, 0):
            for dy in (2, 1, 3, 0):
                if dy or dz:
                    send(src, buf.at[dy * 4 + dz - 1], device(at_y(dy), at_zh(dz), x, zl, c), s)
        pending.append(lambda: wait_bytes(buf, ssem.at[s]))
        return lambda: wait_bytes(buf, rsem.at[s])

    def proto_send(src, buf):
        s = sem()

        def body(i, carry):
            k = 31 - i
            dx, dl, dc = k // 8, (k // 2) % 4, k % 2
            fl = lax.rem(zl + dl, 4)
            send(src, buf.at[k - 1], device(y, zh, at_x(dx), fl, lax.rem(c + dc, 2)), s)
            return carry

        lax.fori_loop(0, 31, body, 0)
        pending.append(lambda: wait_bytes(buf, ssem.at[s]))
        return lambda: wait_bytes(buf, rsem.at[s])

    near = [device(at_y(d), zh, x, zl, c) for d in (1, 2, 3)]
    near += [device(y, at_zh(d), x, zl, c) for d in (1, 2, 3)]
    near += [device(y, zh, x, lax.rem(zl + d, 4), c) for d in (1, 2, 3)]
    near += [
        device(y, zh, at_x(d), zl, lax.rem(c + e, 2))
        for d in range(4) for e in range(2) if d or e
    ]
    barrier = pltpu.get_barrier_semaphore()
    for dev in near:
        pl.semaphore_signal(barrier, inc=1, device_id=dev, device_id_type=MESH)

    def own(block, size):
        return pl.ds(pl.multiple_of(block * size, 16), size)

    wt[own(b, 96), :] = tw[...]
    ws[own(b, 64), :] = sw[...]
    pl.semaphore_wait(barrier, len(near))
    def gather(full, rows, width):
        half = rows // 2

        def part(dy, dz, h, k):
            start = (at_y(dy) * 4 + at_zh(dz)) * rows + h * half
            return full.at[pl.ds(pl.multiple_of(start, 16), half), pl.ds(k * width, width)]

        zc, yc = {}, {}
        ks = range(COLS // width)

        def zs(dz, h, way, k):
            ref = part(0, dz, h, k)
            zc[dz, h, way, k] = single(ref, ref, device(y, at_zh(way), x, zl, c))

        def ys(dy, dz, h, way, k):
            ref = part(dy, dz, h, k)
            yc[dy, dz, h, way, k] = single(ref, ref, device(at_y(way), zh, x, zl, c))

        def start():
            for way, h in ((1, 0), (3, 1), (1, 1), (3, 0)):
                for k in ks:
                    zs(0, h, way, k)

        def both(dz, h, k):
            ys(0, dz, h, 1, k)
            ys(0, dz, h, 3, k)

        def forward(dz, h, k):
            way, source = ((1, 3), (3, 1))[h]
            yc[0, dz, h, way, k].wait_recv()
            ys(source, dz, h, way, k)

        def first(h, k):
            way, source = ((1, 3), (3, 1))[h]
            zc[0, h, way, k].wait_recv()
            both(source, h, k)
            zs(source, h, way, k)

        def second(h, k):
            way, source = ((3, 1), (1, 3))[h]
            zc[0, h, way, k].wait_recv()
            both(source, h, k)

        def third(h, k):
            way, source = ((1, 3), (3, 1))[h]
            zc[source, h, way, k].wait_recv()
            both(2, h, k)

        def finish():
            for dz in (0, 3, 1, 2):
                for k in ks:
                    yc[0, dz, 1, 1, k].wait_recv()
                    yc[0, dz, 0, 3, k].wait_recv()
                    yc[3, dz, 0, 1, k].wait_recv()
                    yc[1, dz, 1, 3, k].wait_recv()

        return start, both, forward, first, second, third, finish

    t_start, t_both, t_forward, t_first, t_second, t_third, t_finish = gather(wt, 96, TPIECE)
    s_start, s_both, s_forward, s_first, s_second, s_third, s_finish = gather(ws, 64, COLS)
    tks = range(COLS // TPIECE)

    for k in tks:
        t_both(0, 0, k)
        t_both(0, 1, k)
    t_start()
    slice_rows = pl.ds(pl.multiple_of((2 * x + c) * 64, 64), 64)
    swap = single(sf.at[slice_rows, :], sf2.at[slice_rows, :], device(at_y(2), zh, x, zl, c))

    fetch.wait()

    def teacher_rows(i, carry):
        rows = pl.ds(pl.multiple_of(i * 128, 128), 128)
        wide = tf[rows, :].astype(F32)
        scale = lax.rsqrt(jnp.sum(wide * wide, axis=1, keepdims=True) + 1e-06)
        tu[rows, :] = (wide * scale).astype(BF16)
        return carry

    lax.fori_loop(0, 4, teacher_rows, 0)

    swap.wait_recv()
    s_feats = sem()
    for d in range(4):
        for e in range(2):
            if d or e:
                send(
                    sf2.at[slice_rows, :], sf2.at[slice_rows, :],
                    device(y, zh, at_x(d), zl, lax.rem(c + e, 2)), s_feats,
                )
    rest = sf2.at[pl.ds(0, 448), :]
    pending.append(lambda: wait_bytes(rest, ssem.at[s_feats]))

    for k in tks:
        t_forward(0, 0, k)
        t_forward(0, 1, k)
    for k in tks:
        t_first(0, k)
        t_first(1, k)
    for k in tks:
        t_forward(3, 0, k)
        t_forward(1, 1, k)
    for k in tks:
        t_second(1, k)
        t_second(0, k)
    for k in tks:
        t_third(0, k)
        t_third(1, k)
        t_forward(3, 1, k)
        t_forward(1, 0, k)
    s_start()
    for k in tks:
        t_forward(2, 0, k)
        t_forward(2, 1, k)
    t_finish()
    def score_cols(j, carry):
        cols = pl.ds(pl.multiple_of(j * 256, 256), 256)
        scores = jnp.dot(tu[...], wt[:, cols], preferred_element_type=F32)
        block = jnp.exp(scores / TEACHER_TEMP)
        mass[:, cols] = block
        colmsg[0, :, cols] = jnp.sum(block, axis=0, keepdims=True)
        return carry

    lax.fori_loop(0, 4, score_cols, 0)

    def by_columns(factor, after):
        def body(i, carry):
            rows = pl.ds(pl.multiple_of(i * 64, 64), 64)
            part = jnp.zeros((64, 128), F32)
            for t in range(8):
                cols = slice(128 * t, 128 * t + 128)
                block = mass[rows, cols] * factor[:, cols]
                if after != 1.0:
                    block = block * after
                mass[rows, cols] = block
                part = part + block
            rowpart[rows, :] = part
            return carry

        lax.fori_loop(0, 8, body, 0)
        return lanes(rowpart[...])

    def by_rows(factor):
        rowb[...] = jnp.broadcast_to(factor, (128, ROWS)).T

        def body(i, carry):
            rows = pl.ds(pl.multiple_of(i * 64, 64), 64)
            by = rowb[rows, :]
            out = []
            for t in range(8):
                cols = slice(128 * t, 128 * t + 128)
                block = mass[rows, cols] * by
                mass[rows, cols] = block
                out.append(carry[t] + jnp.sum(block.reshape(8, 8, 128), axis=0))
            return tuple(out)

        sums = lax.fori_loop(0, 8, body, tuple(jnp.zeros((8, 128), F32) for _ in range(8)))
        return jnp.concatenate([jnp.sum(s, axis=0, keepdims=True) for s in sums], axis=1)

    def total_of(msg, buf):
        return msg + jnp.sum(buf[...], axis=0)

    def student_rows(i, carry):
        rows = pl.ds(pl.multiple_of(i * 128, 128), 128)
        wide = sf2[rows, :].astype(F32)
        scale = lax.rsqrt(jnp.sum(wide * wide, axis=1, keepdims=True) + 1e-06)
        unit = wide * scale
        sh[rows, :] = unit.astype(BF16)
        sht[:, rows] = unit.T.astype(BF16)
        return carry

    def student_logits():
        def body(j, carry):
            cols = pl.ds(pl.multiple_of(j * 256, 256), 256)
            block = jnp.dot(sh[...], ws[:, cols], preferred_element_type=F32) / STUDENT_TEMP
            grown = jnp.exp(block)
            logit[:, cols] = block
            expo[:, cols] = grown
            part = grown[:, :128] + grown[:, 128:]
            totpart[...] = jnp.where(j == 0, part, totpart[...] + part)
            return carry

        lax.fori_loop(0, 4, body, 0)

    def student_near():
        s_first(0, 0)
        s_first(1, 0)
        s_forward(0, 0, 0)
        s_forward(0, 1, 0)
        s_second(1, 0)
        s_second(0, 0)

    def student_far():
        s_third(0, 0)
        s_third(1, 0)
        s_forward(3, 0, 0)
        s_forward(1, 1, 0)
        s_forward(3, 1, 0)
        s_forward(1, 0, 0)

    def student_last():
        s_forward(2, 0, 0)
        s_forward(2, 1, 0)

    def student_end():
        s_finish()
        student_logits()
    for step in range(3):
        got = batch_send(colmsg.at[step], colbuf.at[step])
        if step == 0:
            s_both(0, 0, 0)
            s_both(0, 1, 0)
            wait_bytes(rest, rsem.at[s_feats])
            lax.fori_loop(0, 4, student_rows, 0)
            student_near()
        if step == 1:
            student_far()
        if step == 2:
            student_end()
            lastmsg[:, 512:] = lanes(totpart[...])
        got()
        col_total = total_of(colmsg[step], colbuf.at[step]) * PROTOS
        if step == 0:
            factor = 1.0 / (col_total * 0.25)
            row_sum = by_columns(factor, 0.25)
        else:
            row_sum = by_columns(1.0 / col_total, 1.0)
        if step < 2:
            rowmsg[step] = row_sum
            got = proto_send(rowmsg.at[step], rowbuf.at[step])
            if step == 1:
                student_last()
            got()
            row_total = total_of(rowmsg[step], rowbuf.at[step])
            colmsg[step + 1] = by_rows(1.0 / (CROPS * row_total))
        else:
            lastmsg[:, :512] = row_sum
            got = proto_send(lastmsg, lastbuf)
            got()
    both = total_of(lastmsg[...], lastbuf)
    row_total, total = both[:, :512], both[:, 512:]
    target_factor = CROPS * (1.0 / (CROPS * row_total))
    weight_sum = target_factor * row_total
    rowb[...] = jnp.broadcast_to(target_factor, (128, ROWS)).T
    probb[...] = jnp.broadcast_to(weight_sum * inverse(total, GAIN), (128, ROWS)).T
    crop_term = jnp.sum(weight_sum * jnp.log(total), axis=1, keepdims=True) / 32.0
    def slope_rows(i, carry):
        rows = pl.ds(pl.multiple_of(i * 64, 64), 64)
        by, prob = rowb[rows, :], probb[rows, :]
        for t in range(8):
            cols = slice(128 * t, 128 * t + 128)
            target = mass[rows, cols] * by
            slope[rows, cols] = (expo[rows, cols] * prob - target * GAIN).astype(BF16)
            carry = carry + jnp.sum((target * logit[rows, cols]).reshape(8, 8, 128), axis=0)
        return carry

    pairs = lax.fori_loop(0, 8, slope_rows, jnp.zeros((8, 128), F32))
    pairs = jnp.sum(jnp.sum(pairs, axis=0, keepdims=True), axis=1, keepdims=True)
    lossmsg[0] = jnp.broadcast_to(crop_term - pairs, (1, 128))
    def back_half(half, store):
        rows = pl.ds(pl.multiple_of(half * 256, 256), 256)

        def body(j, carry):
            feats = pl.ds(pl.multiple_of(j * 256, 256), 256)
            store(feats, nt(slope[rows, :], ws[feats, :]))
            return carry

        lax.fori_loop(0, 4, body, 0)

    def store_send(feats, value):
        bsend[:, feats] = value.astype(BF16)

    def store_own(feats, value):
        bown[:, feats] = value

    back_half(1 - c, store_send)
    core_copy = single(bsend, brecv, device(y, zh, x, zl, 1 - c))

    up, down = device(at_y(1), zh, x, zl, c), device(at_y(3), zh, x, zl, c)
    ysent, yfwd = {}, {}

    def weight_made(q):
        cols = slice(256 * q, 256 * q + 256)
        for dy in (2, 1, 3, 0):
            rows = pl.ds(pl.multiple_of(at_y(dy) * 256, 256), 256)
            value = jnp.dot(sht[rows, :], slope[:, cols], preferred_element_type=F32)
            if dy == 2:
                gsend[q, 0] = value[:128].astype(BF16)
                gsend[q, 1] = value[128:].astype(BF16)
            elif dy == 1:
                gkeep[q, 0] = value[:128]
                gsend[q, 2] = value[128:].astype(BF16)
            elif dy == 3:
                gsend[q, 3] = value[:128].astype(BF16)
                gkeep[q, 1] = value[128:]
            else:
                gown[q] = value

    def weight_send(q):
        ysent[q] = [
            single(gsend.at[q, i], grecv.at[q, i], (up, down)[i % 2]) for i in range(4)
        ]

    def weight_forward(q):
        for i in range(2):
            ysent[q][i].wait_recv()
            gsend[q, 4 + i] = (gkeep[q, i] + grecv[q, i].astype(F32)).astype(BF16)
            yfwd[q, i] = single(gsend.at[q, 4 + i], grecv.at[q, 4 + i], (up, down)[i])

    weight_made(0)
    weight_send(0)
    back_half(c, store_own)
    weight_made(1)
    loss_got = proto_send(lossmsg.at[0], lossrow)

    core_copy.wait_recv()
    xcopies = []
    for d in (2, 1, 3):
        rows = pl.ds(pl.multiple_of(at_x(d) * 64, 64), 64)
        xsend[d - 1] = (bown[rows, :] + brecv[rows, :].astype(F32)).astype(BF16)
        xcopies.append(single(xsend.at[d - 1], xrecv.at[d - 1], device(y, zh, at_x(d), zl, c)))

    front, rear = device(y, at_zh(1), x, zl, c), device(y, at_zh(3), x, zl, c)
    zsent, zfwd = {}, {}

    def weight_piece(q, dz, h):
        return gown[q, pl.ds(pl.multiple_of(at_zh(dz) * 64 + h * 32, 32), 32), :]

    def weight_z(q):
        ysent[q][2].wait_recv()
        ysent[q][3].wait_recv()
        yfwd[q, 0].wait_recv()
        yfwd[q, 1].wait_recv()
        low = gown[q, :128] + grecv[q, 3].astype(F32) + grecv[q, 4].astype(F32)
        high = gown[q, 128:] + grecv[q, 2].astype(F32) + grecv[q, 5].astype(F32)
        gown[q, :128] = low
        gown[q, 128:] = high
        for i, (dz, h) in enumerate(((2, 0), (2, 1), (1, 1), (3, 0))):
            zsend[q, i] = weight_piece(q, dz, h).astype(BF16)
        zsent[q] = [
            single(zsend.at[q, i], zrecv.at[q, i], (front, rear)[i % 2]) for i in range(4)
        ]

    def weight_pass(q):
        for i in range(2):
            zsent[q][i].wait_recv()
            kept = weight_piece(q, (1, 3)[i], i)
            zsend[q, 4 + i] = (kept + zrecv[q, i].astype(F32)).astype(BF16)
            zfwd[q, i] = single(zsend.at[q, 4 + i], zrecv.at[q, 4 + i], (front, rear)[i])

    weight_forward(0)
    weight_send(1)
    weight_made(2)
    weight_z(0)
    weight_forward(1)
    weight_send(2)
    weight_made(3)

    for copy in xcopies:
        copy.wait_recv()
    rows = pl.ds(pl.multiple_of(x * 64, 64), 64)
    xsum = bown[rows, :] + brecv[rows, :].astype(F32)
    for d in range(3):
        xsum = xsum + xrecv[d].astype(F32)
    bown[pl.ds(0, 64), :] = xsum
    lcopies = []
    for d in (2, 1, 3):
        fl = lax.rem(zl + d, 4)
        rows = pl.ds(pl.multiple_of(fl * 16, 16), 16)
        lsend[d - 1] = bown[rows, :].astype(BF16)
        lcopies.append(single(lsend.at[d - 1], lrecv.at[d - 1], device(y, zh, x, fl, c)))
    weight_z(1)
    weight_forward(2)
    weight_send(3)
    loss_got()
    lossmsg[1] = lossmsg[0] + jnp.sum(lossrow[...], axis=0)
    loss_got = batch_send(lossmsg.at[1], losscol)

    for copy in lcopies:
        copy.wait_recv()
    rows = pl.ds(pl.multiple_of(zl * 16, 16), 16)
    back = bown[rows, :]
    for d in range(3):
        back = back + lrecv[d].astype(F32)
    mine = pl.ds(pl.multiple_of(c * 256 + x * 64 + zl * 16, 16), 16)
    wide = sf2[mine, :].astype(F32)
    scale = lax.rsqrt(jnp.sum(wide * wide, axis=1, keepdims=True) + 1e-06)
    unit = wide * scale
    inner = jnp.sum(unit * back, axis=1, keepdims=True)
    gfin[...] = ((back - unit * inner) * scale).astype(BF16)
    fcopies = []
    for d in range(4):
        fl = lax.rem(zl + d, 4)
        fcopies.append(single(gfin, gfs.at[mine, :], device(at_y(2), zh, x, fl, c)))
    weight_pass(0)
    weight_z(2)
    weight_forward(3)
    weight_pass(1)

    for copy in fcopies:
        copy.wait_recv()

    def piece(dx, core):
        return gfs.at[pl.ds(pl.multiple_of(core * 256 + at_x(dx) * 64, 64), 64), :]

    lastx = []
    for d in (2, 1, 3):
        lastx.append(single(piece(0, c), piece(0, c), device(y, zh, at_x(d), zl, c)))
    lastc = [single(piece(0, c), piece(0, c), device(y, zh, x, zl, 1 - c))]
    weight_z(3)
    weight_pass(2)

    for d, copy in zip((2, 1, 3), lastx):
        copy.wait_recv()
        lastc.append(single(piece(4 - d, c), piece(4 - d, c), device(y, zh, x, zl, 1 - c)))

    weight_pass(3)
    for q in range(4):
        cols = slice(256 * q, 256 * q + 256)
        zsent[q][2].wait_recv()
        zsent[q][3].wait_recv()
        zfwd[q, 0].wait_recv()
        zfwd[q, 1].wait_recv()
        low = weight_piece(q, 0, 0) + zrecv[q, 3].astype(F32) + zrecv[q, 4].astype(F32)
        high = weight_piece(q, 0, 1) + zrecv[q, 2].astype(F32) + zrecv[q, 5].astype(F32)
        gw_out[:32, cols] = low.astype(BF16)
        gw_out[32:, cols] = high.astype(BF16)

    loss_got()
    loss_out[...] = (lossmsg[1] + jnp.sum(losscol[...], axis=0)) / CROPS

    for copy in lastc:
        copy.wait_recv()
    gf_out[...] = gfs[...]
    for done in pending:
        done()


def shards(teacher_feats, teacher_weight, student_feats, student_weight):
    vm = pltpu.VMEM
    spec = pl.BlockSpec(memory_space=pltpu.VMEM)
    away = pl.BlockSpec(memory_space=pl.ANY)
    loss, grad_weight, grad_feats = pl.pallas_call(
        kernel,
        out_shape=(
            jax.ShapeDtypeStruct((1, 128), F32),
            vm((64, COLS), BF16),
            vm((ROWS, DS), BF16),
        ),
        in_specs=[away, spec, away, spec],
        out_specs=(spec,) * 3,
        scratch_shapes=[
            vm((ROWS, DT), BF16),
            vm((ROWS, DT), BF16),
            vm((DT, COLS), BF16),
            vm((DS, COLS), BF16),
            vm((ROWS, DS), BF16),
            vm((ROWS, DS), BF16),
            vm((DS, ROWS), BF16),
            vm((ROWS, COLS), F32),
            vm((ROWS, COLS), F32),
            vm((ROWS, COLS), F32),
            vm((ROWS, COLS), BF16),
            vm((ROWS, 128), F32),
            vm((ROWS, 128), F32),
            vm((ROWS, 128), F32),
            vm((ROWS, 128), F32),
            vm((3, 1, COLS), F32),
            vm((3, 15, 1, COLS), F32),
            vm((2, 1, ROWS), F32),
            vm((2, 31, 1, ROWS), F32),
            vm((1, 2 * ROWS), F32),
            vm((31, 1, 2 * ROWS), F32),
            vm((2, 1, 128), F32),
            vm((31, 1, 128), F32),
            vm((15, 1, 128), F32),
            vm((256, DS), BF16),
            vm((256, DS), F32),
            vm((256, DS), BF16),
            vm((3, 64, DS), BF16),
            vm((3, 64, DS), BF16),
            vm((3, 16, DS), BF16),
            vm((3, 16, DS), BF16),
            vm((16, DS), BF16),
            vm((ROWS, DS), BF16),
            vm((4, 6, 128, 256), BF16),
            vm((4, 2, 128, 256), F32),
            vm((4, 256, 256), F32),
            vm((4, 6, 128, 256), BF16),
            vm((4, 6, 32, 256), BF16),
            vm((4, 6, 32, 256), BF16),
            pltpu.SemaphoreType.DMA((NSEM,)),
            pltpu.SemaphoreType.DMA((NSEM,)),
            pltpu.SemaphoreType.DMA,
        ],
        compiler_params=pltpu.CompilerParams(
            collective_id=0, has_side_effects=True, vmem_limit_bytes=56 * 2**20
        ),
    )(teacher_feats, teacher_weight, student_feats, student_weight)
    return (loss[0, 0], grad_weight, grad_feats)


def solution(mesh):
    return jax.shard_map(
        shards,
        mesh=mesh,
        in_specs=(P("batch", None), P("batch", "proto"), P("batch", None), P("batch", "proto")),
        out_specs=(P(), P("batch", "proto"), P("batch", None)),
        check_vma=False,
    )
```

```python
import jax
import jax.numpy as jnp
from jax import lax
from jax.experimental import pallas as pl
from jax.experimental.pallas import tpu as pltpu
from jax.sharding import PartitionSpec as P

F32 = jnp.float32
BF16 = jnp.bfloat16
MESH = pl.DeviceIdType.MESH

TEACHER_TEMP = 0.07
STUDENT_TEMP = 0.1
LOSS_SCALE = 1024.0
CROPS = 8192.0
PROTOS = 32768.0
GAIN = LOSS_SCALE / STUDENT_TEMP

ROWS = 512
COLS = 1024
DT = 1536
DS = 1024
NSEM = 256
TPIECE = 1024


def device(y, zh, x, zl, c):
    return (y * 4 + zh, (x * 4 + zl) * 2 + c)


def nt(a, b):
    return lax.dot_general(a, b, (((1,), (1,)), ((), ())), preferred_element_type=F32)


def lanes(part):
    ones = jnp.ones((8, 128), F32)
    out = lax.dot_general(
        ones, part, (((1,), (1,)), ((), ())),
        precision=lax.Precision.HIGHEST, preferred_element_type=F32,
    )
    return out[0:1, :]


def inverse(value, gain):
    part = jnp.where(value > 1.0, 0.25, 1.0)
    return (1.0 / (value * part)) * (part * gain)


def kernel(
    tf_in, tw, sf, sw, loss_out, gw_out, gf_out,
    tf,
    tu, wt, ws, sf2, sh, sht, mass, logit, expo, slope,
    rowpart, totpart, rowb, probb,
    colmsg, colbuf, rowmsg, rowbuf, lastmsg, lastbuf,
    lossmsg, lossrow, losscol,
    bsend, bown, brecv, xsend, xrecv, lsend, lrecv, gfin, gfs,
    gsend, gkeep, gown, grecv, zsend, zrecv,
    ssem, rsem, isem,
):
    b = lax.axis_index("batch")
    p = lax.axis_index("proto")
    y, zh = b // 4, b % 4
    x, zl, c = p // 8, (p // 2) % 4, p % 2

    def at_y(d):
        return lax.rem(y + d, 4)

    def at_zh(d):
        return lax.rem(zh + d, 4)

    def at_x(d):
        return lax.rem(x + d, 4)

    fetch = pltpu.make_async_copy(tf_in, tf, isem)
    fetch.start()

    used = [0]
    pending = []

    def sem():
        used[0] += 1
        return used[0] - 1

    def send(src, dst, dev, s=None, r=None):
        s = sem() if s is None else s
        r = s if r is None else r
        copy = pltpu.make_async_remote_copy(
            src_ref=src, dst_ref=dst, send_sem=ssem.at[s], recv_sem=rsem.at[r],
            device_id=dev, device_id_type=MESH,
        )
        copy.start()
        return copy

    def single(src, dst, dev):
        copy = send(src, dst, dev)
        pending.append(copy.wait_send)
        return copy

    def wait_bytes(ref, s):
        pltpu.make_async_copy(ref, ref, s).wait()

    def batch_send(src, buf):
        s = sem()
        for dz in (2, 1, 3, 0):
            for dy in (2, 1, 3, 0):
                if dy or dz:
                    send(src, buf.at[dy * 4 + dz - 1], device(at_y(dy), at_zh(dz), x, zl, c), s)
        pending.append(lambda: wait_bytes(buf, ssem.at[s]))
        return lambda: wait_bytes(buf, rsem.at[s])

    def proto_send(src, buf):
        s = sem()

        def body(i, carry):
            k = 31 - i
            dx, dl, dc = k // 8, (k // 2) % 4, k % 2
            fl = lax.rem(zl + dl, 4)
            send(src, buf.at[k - 1], device(y, zh, at_x(dx), fl, lax.rem(c + dc, 2)), s)
            return carry

        lax.fori_loop(0, 31, body, 0)
        pending.append(lambda: wait_bytes(buf, ssem.at[s]))
        return lambda: wait_bytes(buf, rsem.at[s])

    near = [device(at_y(d), zh, x, zl, c) for d in (1, 2, 3)]
    near += [device(y, at_zh(d), x, zl, c) for d in (1, 2, 3)]
    near += [device(y, zh, x, lax.rem(zl + d, 4), c) for d in (1, 2, 3)]
    near += [
        device(y, zh, at_x(d), zl, lax.rem(c + e, 2))
        for d in range(4) for e in range(2) if d or e
    ]
    barrier = pltpu.get_barrier_semaphore()
    for dev in near:
        pl.semaphore_signal(barrier, inc=1, device_id=dev, device_id_type=MESH)

    def own(block, size):
        return pl.ds(pl.multiple_of(block * size, 16), size)

    wt[own(b, 96), :] = tw[...]
    ws[own(b, 64), :] = sw[...]
    pl.semaphore_wait(barrier, len(near))
    def gather(full, rows, width):
        half = rows // 2

        def part(dy, dz, h, k):
            start = (at_y(dy) * 4 + at_zh(dz)) * rows + h * half
            return full.at[pl.ds(pl.multiple_of(start, 16), half), pl.ds(k * width, width)]

        zc, yc = {}, {}
        ks = range(COLS // width)

        def zs(dz, h, way, k):
            ref = part(0, dz, h, k)
            zc[dz, h, way, k] = single(ref, ref, device(y, at_zh(way), x, zl, c))

        def ys(dy, dz, h, way, k):
            ref = part(dy, dz, h, k)
            yc[dy, dz, h, way, k] = single(ref, ref, device(at_y(way), zh, x, zl, c))

        def start():
            for way, h in ((1, 0), (3, 1), (1, 1), (3, 0)):
                for k in ks:
                    zs(0, h, way, k)

        def both(dz, h, k):
            ys(0, dz, h, 1, k)
            ys(0, dz, h, 3, k)

        def forward(dz, h, k):
            way, source = ((1, 3), (3, 1))[h]
            yc[0, dz, h, way, k].wait_recv()
            ys(source, dz, h, way, k)

        def first(h, k):
            way, source = ((1, 3), (3, 1))[h]
            zc[0, h, way, k].wait_recv()
            both(source, h, k)
            zs(source, h, way, k)

        def second(h, k):
            way, source = ((3, 1), (1, 3))[h]
            zc[0, h, way, k].wait_recv()
            both(source, h, k)

        def third(h, k):
            way, source = ((1, 3), (3, 1))[h]
            zc[source, h, way, k].wait_recv()
            both(2, h, k)

        def finish():
            for dz in (0, 3, 1, 2):
                for k in ks:
                    yc[0, dz, 1, 1, k].wait_recv()
                    yc[0, dz, 0, 3, k].wait_recv()
                    yc[3, dz, 0, 1, k].wait_recv()
                    yc[1, dz, 1, 3, k].wait_recv()

        return start, both, forward, first, second, third, finish

    t_start, t_both, t_forward, t_first, t_second, t_third, t_finish = gather(wt, 96, TPIECE)
    s_start, s_both, s_forward, s_first, s_second, s_third, s_finish = gather(ws, 64, COLS)
    tks = range(COLS // TPIECE)

    for k in tks:
        t_both(0, 0, k)
        t_both(0, 1, k)
    t_start()
    slice_rows = pl.ds(pl.multiple_of((2 * x + c) * 64, 64), 64)
    swap = single(sf.at[slice_rows, :], sf2.at[slice_rows, :], device(at_y(2), zh, x, zl, c))

    fetch.wait()

    def teacher_rows(i, carry):
        rows = pl.ds(pl.multiple_of(i * 128, 128), 128)
        wide = tf[rows, :].astype(F32)
        scale = lax.rsqrt(jnp.sum(wide * wide, axis=1, keepdims=True) + 1e-06)
        tu[rows, :] = (wide * scale).astype(BF16)
        return carry

    lax.fori_loop(0, 4, teacher_rows, 0)

    swap.wait_recv()
    s_feats = sem()
    for d in range(4):
        for e in range(2):
            if d or e:
                send(
                    sf2.at[slice_rows, :], sf2.at[slice_rows, :],
                    device(y, zh, at_x(d), zl, lax.rem(c + e, 2)), s_feats,
                )
    rest = sf2.at[pl.ds(0, 448), :]
    pending.append(lambda: wait_bytes(rest, ssem.at[s_feats]))

    for k in tks:
        t_forward(0, 0, k)
        t_forward(0, 1, k)
    for k in tks:
        t_first(0, k)
        t_first(1, k)
    for k in tks:
        t_forward(3, 0, k)
        t_forward(1, 1, k)
    for k in tks:
        t_second(1, k)
        t_second(0, k)
    for k in tks:
        t_forward(3, 1, k)
        t_forward(1, 0, k)
    for k in tks:
        t_third(0, k)
        t_third(1, k)
    for k in tks:
        t_forward(2, 0, k)
        t_forward(2, 1, k)
    s_start()
    t_finish()
    def score_cols(j, carry):
        cols = pl.ds(pl.multiple_of(j * 256, 256), 256)
        scores = jnp.dot(tu[...], wt[:, cols], preferred_element_type=F32)
        block = jnp.exp(scores / TEACHER_TEMP)
        mass[:, cols] = block
        colmsg[0, :, cols] = jnp.sum(block, axis=0, keepdims=True)
        return carry

    lax.fori_loop(0, 4, score_cols, 0)

    def by_columns(factor, after):
        def body(i, carry):
            rows = pl.ds(pl.multiple_of(i * 64, 64), 64)
            part = jnp.zeros((64, 128), F32)
            for t in range(8):
                cols = slice(128 * t, 128 * t + 128)
                block = mass[rows, cols] * factor[:, cols]
                if after != 1.0:
                    block = block * after
                mass[rows, cols] = block
                part = part + block
            rowpart[rows, :] = part
            return carry

        lax.fori_loop(0, 8, body, 0)
        return lanes(rowpart[...])

    def by_rows(factor):
        rowb[...] = jnp.broadcast_to(factor, (128, ROWS)).T

        def body(i, carry):
            rows = pl.ds(pl.multiple_of(i * 64, 64), 64)
            by = rowb[rows, :]
            out = []
            for t in range(8):
                cols = slice(128 * t, 128 * t + 128)
                block = mass[rows, cols] * by
                mass[rows, cols] = block
                out.append(carry[t] + jnp.sum(block.reshape(8, 8, 128), axis=0))
            return tuple(out)

        sums = lax.fori_loop(0, 8, body, tuple(jnp.zeros((8, 128), F32) for _ in range(8)))
        return jnp.concatenate([jnp.sum(s, axis=0, keepdims=True) for s in sums], axis=1)

    def total_of(msg, buf):
        return msg + jnp.sum(buf[...], axis=0)

    def student_rows(i, carry):
        rows = pl.ds(pl.multiple_of(i * 128, 128), 128)
        wide = sf2[rows, :].astype(F32)
        scale = lax.rsqrt(jnp.sum(wide * wide, axis=1, keepdims=True) + 1e-06)
        unit = wide * scale
        sh[rows, :] = unit.astype(BF16)
        sht[:, rows] = unit.T.astype(BF16)
        return carry

    def student_logits():
        def body(j, carry):
            cols = pl.ds(pl.multiple_of(j * 256, 256), 256)
            block = jnp.dot(sh[...], ws[:, cols], preferred_element_type=F32) / STUDENT_TEMP
            grown = jnp.exp(block)
            logit[:, cols] = block
            expo[:, cols] = grown
            part = grown[:, :128] + grown[:, 128:]
            totpart[...] = jnp.where(j == 0, part, totpart[...] + part)
            return carry

        lax.fori_loop(0, 4, body, 0)

    def student_near():
        s_first(0, 0)
        s_first(1, 0)
        s_forward(0, 0, 0)
        s_forward(0, 1, 0)
        s_second(1, 0)
        s_second(0, 0)

    def student_far():
        s_third(0, 0)
        s_third(1, 0)
        s_forward(3, 0, 0)
        s_forward(1, 1, 0)
        s_forward(3, 1, 0)
        s_forward(1, 0, 0)

    def student_last():
        s_forward(2, 0, 0)
        s_forward(2, 1, 0)

    def student_end():
        s_finish()
        student_logits()
    for step in range(3):
        got = batch_send(colmsg.at[step], colbuf.at[step])
        if step == 0:
            s_both(0, 0, 0)
            s_both(0, 1, 0)
            wait_bytes(rest, rsem.at[s_feats])
            lax.fori_loop(0, 4, student_rows, 0)
            student_near()
        if step == 1:
            student_far()
        if step == 2:
            student_end()
            lastmsg[:, 512:] = lanes(totpart[...])
        got()
        col_total = total_of(colmsg[step], colbuf.at[step]) * PROTOS
        if step == 0:
            factor = 1.0 / (col_total * 0.25)
            row_sum = by_columns(factor, 0.25)
        else:
            row_sum = by_columns(1.0 / col_total, 1.0)
        if step < 2:
            rowmsg[step] = row_sum
            got = proto_send(rowmsg.at[step], rowbuf.at[step])
            if step == 1:
                student_last()
            got()
            row_total = total_of(rowmsg[step], rowbuf.at[step])
            colmsg[step + 1] = by_rows(1.0 / (CROPS * row_total))
        else:
            lastmsg[:, :512] = row_sum
            got = proto_send(lastmsg, lastbuf)
            got()
    both = total_of(lastmsg[...], lastbuf)
    row_total, total = both[:, :512], both[:, 512:]
    target_factor = CROPS * (1.0 / (CROPS * row_total))
    weight_sum = target_factor * row_total
    rowb[...] = jnp.broadcast_to(target_factor, (128, ROWS)).T
    probb[...] = jnp.broadcast_to(weight_sum * inverse(total, GAIN), (128, ROWS)).T
    crop_term = jnp.sum(weight_sum * jnp.log(total), axis=1, keepdims=True) / 32.0
    def slope_rows(i, carry):
        rows = pl.ds(pl.multiple_of(i * 64, 64), 64)
        by, prob = rowb[rows, :], probb[rows, :]
        for t in range(8):
            cols = slice(128 * t, 128 * t + 128)
            target = mass[rows, cols] * by
            slope[rows, cols] = (expo[rows, cols] * prob - target * GAIN).astype(BF16)
            carry = carry + jnp.sum((target * logit[rows, cols]).reshape(8, 8, 128), axis=0)
        return carry

    pairs = lax.fori_loop(0, 8, slope_rows, jnp.zeros((8, 128), F32))
    pairs = jnp.sum(jnp.sum(pairs, axis=0, keepdims=True), axis=1, keepdims=True)
    lossmsg[0] = jnp.broadcast_to(crop_term - pairs, (1, 128))
    def back_half(half, store):
        rows = pl.ds(pl.multiple_of(half * 256, 256), 256)

        def body(j, carry):
            feats = pl.ds(pl.multiple_of(j * 256, 256), 256)
            store(feats, nt(slope[rows, :], ws[feats, :]))
            return carry

        lax.fori_loop(0, 4, body, 0)

    def store_send(feats, value):
        bsend[:, feats] = value.astype(BF16)

    def store_own(feats, value):
        bown[:, feats] = value

    back_half(1 - c, store_send)
    core_copy = single(bsend, brecv, device(y, zh, x, zl, 1 - c))

    up, down = device(at_y(1), zh, x, zl, c), device(at_y(3), zh, x, zl, c)
    ysent, yfwd = {}, {}

    def weight_made(q):
        cols = slice(256 * q, 256 * q + 256)
        for dy in (2, 1, 3, 0):
            rows = pl.ds(pl.multiple_of(at_y(dy) * 256, 256), 256)
            value = jnp.dot(sht[rows, :], slope[:, cols], preferred_element_type=F32)
            if dy == 2:
                gsend[q, 0] = value[:128].astype(BF16)
                gsend[q, 1] = value[128:].astype(BF16)
            elif dy == 1:
                gkeep[q, 0] = value[:128]
                gsend[q, 2] = value[128:].astype(BF16)
            elif dy == 3:
                gsend[q, 3] = value[:128].astype(BF16)
                gkeep[q, 1] = value[128:]
            else:
                gown[q] = value

    def weight_send(q):
        ysent[q] = [
            single(gsend.at[q, i], grecv.at[q, i], (up, down)[i % 2]) for i in range(4)
        ]

    def weight_forward(q):
        for i in range(2):
            ysent[q][i].wait_recv()
            gsend[q, 4 + i] = (gkeep[q, i] + grecv[q, i].astype(F32)).astype(BF16)
            yfwd[q, i] = single(gsend.at[q, 4 + i], grecv.at[q, 4 + i], (up, down)[i])

    weight_made(0)
    weight_send(0)
    back_half(c, store_own)
    weight_made(1)

    core_copy.wait_recv()
    xcopies = []
    for d in (2, 1, 3):
        rows = pl.ds(pl.multiple_of(at_x(d) * 64, 64), 64)
        xsend[d - 1] = (bown[rows, :] + brecv[rows, :].astype(F32)).astype(BF16)
        xcopies.append(single(xsend.at[d - 1], xrecv.at[d - 1], device(y, zh, at_x(d), zl, c)))

    loss_got = proto_send(lossmsg.at[0], lossrow)

    front, rear = device(y, at_zh(1), x, zl, c), device(y, at_zh(3), x, zl, c)
    zsent, zfwd = {}, {}

    def weight_piece(q, dz, h):
        return gown[q, pl.ds(pl.multiple_of(at_zh(dz) * 64 + h * 32, 32), 32), :]

    def weight_z(q):
        ysent[q][2].wait_recv()
        ysent[q][3].wait_recv()
        yfwd[q, 0].wait_recv()
        yfwd[q, 1].wait_recv()
        low = gown[q, :128] + grecv[q, 3].astype(F32) + grecv[q, 4].astype(F32)
        high = gown[q, 128:] + grecv[q, 2].astype(F32) + grecv[q, 5].astype(F32)
        gown[q, :128] = low
        gown[q, 128:] = high
        for i, (dz, h) in enumerate(((2, 0), (2, 1), (1, 1), (3, 0))):
            zsend[q, i] = weight_piece(q, dz, h).astype(BF16)
        zsent[q] = [
            single(zsend.at[q, i], zrecv.at[q, i], (front, rear)[i % 2]) for i in range(4)
        ]

    def weight_pass(q):
        for i in range(2):
            zsent[q][i].wait_recv()
            kept = weight_piece(q, (1, 3)[i], i)
            zsend[q, 4 + i] = (kept + zrecv[q, i].astype(F32)).astype(BF16)
            zfwd[q, i] = single(zsend.at[q, 4 + i], zrecv.at[q, 4 + i], (front, rear)[i])

    weight_forward(0)
    weight_send(1)
    weight_made(2)
    weight_z(0)
    weight_forward(1)
    weight_send(2)
    weight_made(3)

    for copy in xcopies:
        copy.wait_recv()
    rows = pl.ds(pl.multiple_of(x * 64, 64), 64)
    xsum = bown[rows, :] + brecv[rows, :].astype(F32)
    for d in range(3):
        xsum = xsum + xrecv[d].astype(F32)
    bown[pl.ds(0, 64), :] = xsum
    lcopies = []
    for d in (2, 1, 3):
        fl = lax.rem(zl + d, 4)
        rows = pl.ds(pl.multiple_of(fl * 16, 16), 16)
        lsend[d - 1] = bown[rows, :].astype(BF16)
        lcopies.append(single(lsend.at[d - 1], lrecv.at[d - 1], device(y, zh, x, fl, c)))
    weight_z(1)
    weight_forward(2)
    weight_send(3)

    for copy in lcopies:
        copy.wait_recv()
    rows = pl.ds(pl.multiple_of(zl * 16, 16), 16)
    back = bown[rows, :]
    for d in range(3):
        back = back + lrecv[d].astype(F32)
    mine = pl.ds(pl.multiple_of(c * 256 + x * 64 + zl * 16, 16), 16)
    wide = sf2[mine, :].astype(F32)
    scale = lax.rsqrt(jnp.sum(wide * wide, axis=1, keepdims=True) + 1e-06)
    unit = wide * scale
    inner = jnp.sum(unit * back, axis=1, keepdims=True)
    gfin[...] = ((back - unit * inner) * scale).astype(BF16)
    fcopies = []
    for d in range(4):
        fl = lax.rem(zl + d, 4)
        fcopies.append(single(gfin, gfs.at[mine, :], device(at_y(2), zh, x, fl, c)))
    loss_got()
    lossmsg[1] = lossmsg[0] + jnp.sum(lossrow[...], axis=0)
    loss_got = batch_send(lossmsg.at[1], losscol)
    weight_pass(0)
    weight_z(2)
    weight_forward(3)
    weight_pass(1)

    for copy in fcopies:
        copy.wait_recv()

    def piece(dx, core):
        return gfs.at[pl.ds(pl.multiple_of(core * 256 + at_x(dx) * 64, 64), 64), :]

    lastx = []
    for d in (2, 1, 3):
        lastx.append(single(piece(0, c), piece(0, c), device(y, zh, at_x(d), zl, c)))
    lastc = [single(piece(0, c), piece(0, c), device(y, zh, x, zl, 1 - c))]
    weight_z(3)
    weight_pass(2)

    for d, copy in zip((2, 1, 3), lastx):
        copy.wait_recv()
        lastc.append(single(piece(4 - d, c), piece(4 - d, c), device(y, zh, x, zl, 1 - c)))

    weight_pass(3)
    for q in range(4):
        cols = slice(256 * q, 256 * q + 256)
        zsent[q][2].wait_recv()
        zsent[q][3].wait_recv()
        zfwd[q, 0].wait_recv()
        zfwd[q, 1].wait_recv()
        low = weight_piece(q, 0, 0) + zrecv[q, 3].astype(F32) + zrecv[q, 4].astype(F32)
        high = weight_piece(q, 0, 1) + zrecv[q, 2].astype(F32) + zrecv[q, 5].astype(F32)
        gw_out[:32, cols] = low.astype(BF16)
        gw_out[32:, cols] = high.astype(BF16)

    loss_got()
    loss_out[...] = (lossmsg[1] + jnp.sum(losscol[...], axis=0)) / CROPS

    for copy in lastc:
        copy.wait_recv()
    gf_out[...] = gfs[...]
    for done in pending:
        done()


def shards(teacher_feats, teacher_weight, student_feats, student_weight):
    vm = pltpu.VMEM
    spec = pl.BlockSpec(memory_space=pltpu.VMEM)
    away = pl.BlockSpec(memory_space=pl.ANY)
    loss, grad_weight, grad_feats = pl.pallas_call(
        kernel,
        out_shape=(
            jax.ShapeDtypeStruct((1, 128), F32),
            vm((64, COLS), BF16),
            vm((ROWS, DS), BF16),
        ),
        in_specs=[away, spec, away, spec],
        out_specs=(spec,) * 3,
        scratch_shapes=[
            vm((ROWS, DT), BF16),
            vm((ROWS, DT), BF16),
            vm((DT, COLS), BF16),
            vm((DS, COLS), BF16),
            vm((ROWS, DS), BF16),
            vm((ROWS, DS), BF16),
            vm((DS, ROWS), BF16),
            vm((ROWS, COLS), F32),
            vm((ROWS, COLS), F32),
            vm((ROWS, COLS), F32),
            vm((ROWS, COLS), BF16),
            vm((ROWS, 128), F32),
            vm((ROWS, 128), F32),
            vm((ROWS, 128), F32),
            vm((ROWS, 128), F32),
            vm((3, 1, COLS), F32),
            vm((3, 15, 1, COLS), F32),
            vm((2, 1, ROWS), F32),
            vm((2, 31, 1, ROWS), F32),
            vm((1, 2 * ROWS), F32),
            vm((31, 1, 2 * ROWS), F32),
            vm((2, 1, 128), F32),
            vm((31, 1, 128), F32),
            vm((15, 1, 128), F32),
            vm((256, DS), BF16),
            vm((256, DS), F32),
            vm((256, DS), BF16),
            vm((3, 64, DS), BF16),
            vm((3, 64, DS), BF16),
            vm((3, 16, DS), BF16),
            vm((3, 16, DS), BF16),
            vm((16, DS), BF16),
            vm((ROWS, DS), BF16),
            vm((4, 6, 128, 256), BF16),
            vm((4, 2, 128, 256), F32),
            vm((4, 256, 256), F32),
            vm((4, 6, 128, 256), BF16),
            vm((4, 6, 32, 256), BF16),
            vm((4, 6, 32, 256), BF16),
            pltpu.SemaphoreType.DMA((NSEM,)),
            pltpu.SemaphoreType.DMA((NSEM,)),
            pltpu.SemaphoreType.DMA,
        ],
        compiler_params=pltpu.CompilerParams(
            collective_id=0, has_side_effects=True, vmem_limit_bytes=56 * 2**20
        ),
    )(teacher_feats, teacher_weight, student_feats, student_weight)
    return (loss[0, 0], grad_weight, grad_feats)


def solution(mesh):
    return jax.shard_map(
        shards,
        mesh=mesh,
        in_specs=(P("batch", None), P("batch", "proto"), P("batch", None), P("batch", "proto")),
        out_specs=(P(), P("batch", "proto"), P("batch", None)),
        check_vma=False,
    )
```
